512 devices in a mesh: dp: 32 (over y_lo, x, core), shard: 16 (over y_hi, z).
Axes of the slice: x: 4, y: 8 (y_hi: 2, y_lo: 4; y = y_hi * 4 + y_lo), z: 8, core: 2. Of those that a mesh axis runs over, the one named last changes fastest.
Arguments:
- residual_in: bfloat16 [24576, 4096], P(('dp', 'shard')), may hold values from -24 to 24
- conv_out: bfloat16 [24576, 8192], P('dp', 'shard'), may hold values from -6 to 6
- b_proj: bfloat16 [24576, 512], P('dp'), may hold values from -2 to 2
- c_proj: bfloat16 [24576, 512], P('dp'), may hold values from -2 to 2
- grad_out: bfloat16 [24576, 8192], P('dp', 'shard'), may hold values from -6 to 6
- doc_starts: int32 [24576], P('dp'), may hold values from 0 to 1, as said below
- dest_plan: int32 [512], P('dp'), may hold values from 0 to 31, as said below
- dt_weight: bfloat16 [4096, 128], P('shard'), may hold values from -0.09375 to 0.09375
- dt_bias: float32 [128], replicated, may hold values from -3 to 0
- decay_rate: float32 [128], replicated, may hold values from 0.02 to 0.5
- skip_gain: float32 [128], replicated, may hold values from 0.5 to 1.5
Outputs:
- conv_grad: bfloat16 [24576, 8192], P('dp', 'shard')
- dt_weight_grad: float32 [4096, 128], P('shard')
The draws below stay inside these ranges and needn't reach their ends.
Inputs may be any that keep to these rules, and one draw needn't show every extreme that they name: `doc_starts`: the first token of every aligned block of 48 tokens is 1; a 1 begins a document, which runs up to the next 1. `dest_plan`: the 16 blocks of one dp index go to 16 different dp indices, and every dp index receives exactly one block in each of its 16 block positions.
All inputs are finite; a program needn't handle non-finite values.
Results may differ from the reference program's by a relative error of at most 0.0043.
Values may be sent and summed in bfloat16 or wider, within the bound.
A program may use at most 64 MiB of HBM per device.

```python
import math
import jax
import jax.numpy as jnp
from jax import lax

D = 4096
H = 128
P_SIZE = 64
N = 128
G = 4
NBLK = 16
BLK = 48
ROWS = 768
TOKENS = 24576
N_DP = 32


def draw_doc_starts(key, part):
    key = jax.random.fold_in(key, 11)
    coins = jax.random.randint(key, (TOKENS,), 0, 12)
    position = jnp.arange(TOKENS)
    return jnp.where((coins == 0) | (position % BLK == 0), 1, 0).astype(jnp.int32)


def draw_dest_plan(key, part):
    key = jax.random.fold_in(key, 23)
    first, second, third = jax.random.split(key, 3)
    relabel = jax.random.permutation(first, N_DP)
    shuffle = jax.random.permutation(second, N_DP)
    offsets = jax.random.permutation(third, N_DP)[:NBLK]
    target = relabel[(shuffle[:, None] + offsets[None, :]) % N_DP]
    return target.reshape(N_DP * NBLK).astype(jnp.int32)


def raised(values, rng, source, target, parts, factor):
    def block_of(dim):
        return (jnp.arange(values.shape[dim]) // (values.shape[dim] // parts)).reshape((-1,) + (1,) * (values.ndim - 1 - dim))

    one_side = jax.random.permutation(rng, parts)[block_of(target)]
    far = (block_of(target) + parts // 2) % parts
    return jnp.where((block_of(source) == one_side) | (block_of(source) == far), factor * values, values)


def level_of(rng, dims, cuts, low, top_value):
    factor_of = 1.0
    for dim, parts in cuts:
        draws = jax.random.uniform(jax.random.fold_in(jax.random.fold_in(rng, 6), dim), (parts,), jnp.float32, low / len(cuts), top_value / len(cuts))
        factor_of = factor_of * jnp.repeat(jnp.exp(draws), dims[dim] // parts).reshape((-1,) + (1,) * (len(dims) - 1 - dim))
    return factor_of


def scatter_about(key, extent, deviation, most, shards=(), kind=jnp.bfloat16):
    level = level_of(key, extent, shards, -0.22, 0.18) if shards else 1.0
    array = jax.random.normal(key, extent, jnp.float32) * deviation * level
    return jnp.minimum(jnp.maximum(array, -most), most).astype(kind)


def gaussian_with(stream_key, extent, scale, reach, shards, heavy, kind=jnp.bfloat16):
    result = scale * jax.random.normal(stream_key, extent, jnp.float32)
    if shards:
        result = result * level_of(stream_key, extent, shards, -0.22, 0.18)
    return jnp.clip(raised(result, jax.random.fold_in(stream_key, 3), *heavy), -reach, reach).astype(kind)


def setup_inputs(seed: int = 0) -> dict:
    streams_of = jax.random.split(jax.random.key(seed), 12)
    residual_in = gaussian_with(streams_of[0], (TOKENS, D), 1.0, 24.0, ((0, 512),), (0, 1, 512, 6.0))
    conv_out = scatter_about(streams_of[1], (TOKENS, H * P_SIZE), 1.0, 6.0, ((0, 32), (1, 16)))
    b_proj = scatter_about(streams_of[2], (TOKENS, G * N), 0.3, 2.0, ((0, 32),))
    c_proj = scatter_about(streams_of[3], (TOKENS, G * N), 0.3, 2.0, ((0, 32),))
    grad_out = scatter_about(streams_of[4], (TOKENS, H * P_SIZE), 1.0, 6.0, ((0, 32), (1, 16)))
    doc_starts = draw_doc_starts(jax.random.fold_in(streams_of[11], 71), 0)
    dest_plan = draw_dest_plan(jax.random.fold_in(streams_of[11], 71), 0)
    dt_weight = scatter_about(streams_of[7], (D, H), D ** -0.5, 0.09375, ((0, 16),))
    dt_bias = jnp.clip(jax.random.uniform(streams_of[8], (H,), jnp.float32, -3.0, 0.0), -3.0, 0.0)
    decay_rate = jnp.clip(jnp.exp(jax.random.uniform(streams_of[9], (H,), jnp.float32, math.log(0.02), math.log(0.5))), 0.02, 0.5)
    skip_gain = jnp.clip(jax.random.uniform(streams_of[10], (H,), jnp.float32, 0.5, 1.5), 0.5, 1.5)
    return dict(residual_in=residual_in, conv_out=conv_out, b_proj=b_proj, c_proj=c_proj, grad_out=grad_out, doc_starts=doc_starts, dest_plan=dest_plan, dt_weight=dt_weight, dt_bias=dt_bias, decay_rate=decay_rate, skip_gain=skip_gain)


def group_grads(pre, values, b_rows, c_rows, starts, upstream, bias, rate, gain, block_len):
    rows, heads = pre.shape
    width = values.shape[1] // heads
    count = rows // block_len
    gate_in = pre + bias[None, :]
    step_size = jax.nn.softplus(gate_in)
    log_decay = -step_size * rate[None, :]
    level = jnp.cumsum(log_decay.reshape(count, block_len, heads), axis=1).transpose(0, 2, 1)
    segment = jnp.cumsum(starts.reshape(count, block_len), axis=1)
    position = jnp.arange(block_len)
    causal = position[:, None] >= position[None, :]
    allowed = (segment[:, :, None] == segment[:, None, :]) & causal[None]
    c_blocks = c_rows.reshape(count, block_len, -1).astype(jnp.float32)
    b_blocks = b_rows.reshape(count, block_len, -1).astype(jnp.float32)
    score = jnp.einsum("cin,cjn->cij", c_blocks, b_blocks)
    steps_t = step_size.reshape(count, block_len, heads).transpose(0, 2, 1)
    spread = level[:, :, :, None] - level[:, :, None, :]
    mask = allowed[:, None]
    decay = jnp.where(mask, jnp.exp(jnp.where(mask, spread, 0.0)), 0.0)
    mixing = (score[:, None] * decay * steps_t[:, :, None, :]).astype(jnp.bfloat16)
    vals = values.reshape(count, block_len, heads, width).astype(jnp.float32)
    ups = upstream.reshape(count, block_len, heads, width).astype(jnp.float32)
    grad_mixing = jnp.einsum("cihp,cjhp->chij", ups, vals)
    grad_values = jnp.einsum("chij,cihp->cjhp", mixing.astype(jnp.float32), ups)
    weighted = grad_mixing * score[:, None] * decay
    grad_step = jnp.sum(weighted, axis=2)
    flow = weighted * steps_t[:, :, None, :]
    grad_level = jnp.sum(flow, axis=3) - jnp.sum(flow, axis=2)
    grad_log = jnp.flip(jnp.cumsum(jnp.flip(grad_level, 2), axis=2), 2)
    combined = grad_step - rate[None, :, None] * grad_log
    grad_pre = combined.transpose(0, 2, 1).reshape(rows, heads) * jax.nn.sigmoid(gate_in)
    grad_conv = grad_values.reshape(rows, heads * width) + jnp.repeat(gain, width)[None, :] * upstream.astype(jnp.float32)
    return grad_conv.astype(jnp.bfloat16), grad_pre


def reference(residual_in, conv_out, b_proj, c_proj, grad_out, doc_starts, dest_plan, dt_weight, dt_bias, decay_rate, skip_gain):
    per_group = H // G

    def one_index(total, item):
        tokens, values, b_rows, c_rows, upstream, starts = item
        pre = jnp.dot(tokens, dt_weight, preferred_element_type=jnp.float32)
        conv_parts = []
        pre_parts = []
        for group in range(G):
            lower = group * per_group
            upper = lower + per_group
            grad_conv, grad_pre = group_grads(pre[:, lower:upper], values[:, lower * P_SIZE:upper * P_SIZE],
                                              b_rows[:, group * N:(group + 1) * N], c_rows[:, group * N:(group + 1) * N],
                                              starts, upstream[:, lower * P_SIZE:upper * P_SIZE], dt_bias[lower:upper],
                                              decay_rate[lower:upper], skip_gain[lower:upper], BLK)
            conv_parts.append(grad_conv)
            pre_parts.append(grad_pre)
        grad_pre_all = jnp.concatenate(pre_parts, axis=1).astype(jnp.bfloat16)
        total = total + jnp.dot(tokens.T, grad_pre_all, preferred_element_type=jnp.float32)
        return total, jnp.concatenate(conv_parts, axis=1)

    total, grad_all = lax.scan(one_index, jnp.zeros((D, H), jnp.float32),
                               (residual_in.reshape(N_DP, ROWS, D), conv_out.reshape(N_DP, ROWS, H * P_SIZE),
                                b_proj.reshape(N_DP, ROWS, G * N), c_proj.reshape(N_DP, ROWS, G * N),
                                grad_out.reshape(N_DP, ROWS, H * P_SIZE), doc_starts.reshape(N_DP, ROWS)))
    grad_blocks = grad_all.reshape(N_DP, NBLK, BLK, H * P_SIZE)
    targets = dest_plan.reshape(N_DP, NBLK).astype(jnp.int32)
    block_index = jnp.broadcast_to(jnp.arange(NBLK, dtype=jnp.int32)[None, :], targets.shape)
    placed = jnp.zeros_like(grad_blocks).at[targets, block_index].set(grad_blocks)
    conv_grad = placed.reshape(TOKENS, H * P_SIZE)
    dt_weight_grad = total * (float(TOKENS) ** -0.5)
    return conv_grad, dt_weight_grad
```

```python
import functools

import jax
import jax.numpy as jnp
from jax import lax
from jax.experimental import pallas as pl
from jax.experimental.pallas import tpu as pltpu
from jax.sharding import PartitionSpec as P

N = 128
G = 4
BLK = 48
LANES = 128
MESH = pl.DeviceIdType.MESH
F32 = jnp.float32
BF16 = jnp.bfloat16
NT = (((1,), (1,)), ((), ()))
NN = (((1,), (0,)), ((), ()))
N_YHI = 2


class Grid:
    def __init__(self, n_dp, n_shard):
        self.n_dp = n_dp
        self.n_z = n_shard // N_YHI
        self.n_core = 2
        rest = n_dp // 2
        self.n_hb = 2 if rest >= 2 else 1
        rest //= self.n_hb
        self.n_x = min(rest, 4)
        self.n_lb = rest // self.n_x
        self.n_y = self.n_hb * self.n_lb

    def here(self):
        dp = lax.axis_index("dp")
        shard = lax.axis_index("shard")
        core = lax.rem(dp, self.n_core)
        x = lax.rem(dp // self.n_core, self.n_x)
        y = dp // (self.n_core * self.n_x)
        return dp, y, x, core, shard // self.n_z, lax.rem(shard, self.n_z)

    def dp_of(self, y, x, core):
        return (y * self.n_x + x) * self.n_core + core

    def partner(self, s):
        _, y, x, core, _, _ = self.here()
        mc = self.n_core - 1 - s % self.n_core
        mx = self.n_x - 1 - (s // self.n_core) % self.n_x
        t = s // (self.n_core * self.n_x)
        hb = y // self.n_lb
        lb = y % self.n_lb
        hb2 = (hb + self.n_hb - 1 + t // self.n_lb) % self.n_hb
        lb2 = (lb + self.n_lb - 1 + t % self.n_lb) % self.n_lb
        if self.n_lb == 1:
            lb2 = lb
        return self.dp_of(hb2 * self.n_lb + lb2, (x + mx) % self.n_x, (core + mc) % self.n_core)

    def source(self, s):
        _, y, x, core, _, _ = self.here()
        mc = self.n_core - 1 - s % self.n_core
        mx = self.n_x - 1 - (s // self.n_core) % self.n_x
        t = s // (self.n_core * self.n_x)
        hb = y // self.n_lb
        lb = y % self.n_lb
        hb2 = (hb + self.n_hb - 1 + t // self.n_lb) % self.n_hb
        lb2 = (lb + self.n_lb - 1 + t % self.n_lb) % self.n_lb
        if self.n_lb == 1:
            lb2 = lb
        return self.dp_of(hb2 * self.n_lb + lb2, (x + self.n_x - mx) % self.n_x, (core + mc) % self.n_core)


def remote(src, dst, send, recv, device):
    return pltpu.make_async_remote_copy(
        src_ref=src, dst_ref=dst, send_sem=send, recv_sem=recv, device_id=device, device_id_type=MESH
    )


def spread_lanes(whole, index):
    width = whole.shape[1]
    low = index * BLK
    if width % LANES:
        return jnp.pad(whole[:, low : low + BLK], ((0, 0), (0, LANES - BLK)))
    tile, off = low // LANES, low % LANES
    first = whole[:, tile * LANES : (tile + 1) * LANES]
    if off == 0:
        return first
    first = pltpu.roll(first, LANES - off, 1)
    if off + BLK <= LANES:
        return first
    second = pltpu.roll(whole[:, (tile + 1) * LANES : (tile + 2) * LANES], LANES - off, 1)
    lane = lax.broadcasted_iota(jnp.int32, first.shape, 1)
    return jnp.where(lane < LANES - off, first, second)


def gather_lanes(pieces):
    count = len(pieces)
    width = count * BLK
    if width % LANES:
        return jnp.concatenate([p[:, :BLK] for p in pieces], axis=1)
    lane = lax.broadcasted_iota(jnp.int32, (8, LANES), 1)
    tiles = [jnp.zeros((8, LANES), F32) for _ in range(width // LANES)]
    for index, piece in enumerate(pieces):
        low = index * BLK
        tile, off = low // LANES, low % LANES
        moved = pltpu.roll(piece, off, 1) if off else piece
        tiles[tile] = jnp.where((lane >= off) & (lane < off + BLK), moved, tiles[tile])
        if off + BLK > LANES:
            tiles[tile + 1] = jnp.where(lane < off + BLK - LANES, moved, tiles[tile + 1])
    return jnp.concatenate(tiles, axis=1)


def project_kernel(
    grid, x_ref, w_ref, xg_ref, pre_ref, wo_ref, full_ref, part_ref, rs_ref, give_ref, take_ref,
    xs_sem, xr_sem, ws_sem, wr_sem, ps_sem, pr_sem, ss_sem, sr_sem, local_sem,
):
    n_z = grid.n_z
    _, _, _, _, yh, z = grid.here()
    half = n_z * BLK
    feats = w_ref.shape[0]

    def peer(step):
        return {"shard": yh * n_z + (z + step) % n_z}

    across = {"shard": (1 - yh) * n_z + z}
    barrier = pltpu.get_barrier_semaphore()
    for step in range(1, n_z):
        pl.semaphore_signal(barrier, inc=1, device_id=peer(step), device_id_type=MESH)
    pl.semaphore_signal(barrier, inc=1, device_id=across, device_id_type=MESH)

    def columns(side, step):
        owner = (yh if side == 0 else 1 - yh) * n_z + (z + step) % n_z
        return x_ref.at[:, pl.ds(pl.multiple_of(owner * feats, feats), feats)]

    mine = pl.ds(pl.multiple_of(z * BLK, BLK), BLK)
    own = [pltpu.make_async_copy(columns(side, 0), xg_ref.at[side, mine], local_sem.at[side]) for side in range(2)]
    for copy in own:
        copy.start()
    pl.semaphore_wait(barrier, n_z)
    copies = []
    swap = remote(w_ref, wo_ref, ws_sem, wr_sem, across)
    swap.start()
    for step in range(1, n_z):
        for side in range(2):
            copy = remote(
                columns(side, step), xg_ref.at[side, mine],
                xs_sem.at[step, side], xr_sem.at[step, side], peer(step),
            )
            copy.start()
            copies.append(copy)
    w_here = w_ref[...].astype(F32).T.astype(BF16)
    for copy in own:
        copy.wait()
    swap.wait()
    w_other = wo_ref[...].astype(F32).T.astype(BF16)
    for copy in copies:
        copy.wait()
    full_ref[...] = lax.dot_general(w_here, xg_ref[0], NT, preferred_element_type=F32) + lax.dot_general(
        w_other, xg_ref[1], NT, preferred_element_type=F32
    )
    copies = []
    for step in list(range(1, n_z)) + [0]:
        for side in range(2):
            owner = (yh if side == 0 else 1 - yh) * n_z + (z + step) % n_z
            part_ref[step, side * 8 : (side + 1) * 8] = full_ref[pl.ds(pl.multiple_of(owner * 8, 8), 8)]
        if step:
            copy = remote(part_ref.at[step], rs_ref.at[step], ps_sem.at[step], pr_sem.at[step], peer(step))
            copy.start()
            copies.append(copy)
    total = part_ref[0]
    for step, copy in enumerate(copies, 1):
        copy.wait()
        total = total + rs_ref[step]
    give_ref[...] = total[8:]
    swap = remote(give_ref, take_ref, ss_sem, sr_sem, across)
    swap.start()
    for block in range(n_z):
        pre_ref[yh * n_z + block] = spread_lanes(total[:8], block)
    swap.wait()
    other = take_ref[...]
    for block in range(n_z):
        pre_ref[(1 - yh) * n_z + block] = spread_lanes(other, block)


def project(grid, tokens, weight):
    n_z = grid.n_z
    half = n_z * BLK
    feats, heads = weight.shape
    dma = pltpu.SemaphoreType.DMA
    return pl.pallas_call(
        functools.partial(project_kernel, grid),
        out_shape=(
            jax.ShapeDtypeStruct((2, half, feats), BF16),
            jax.ShapeDtypeStruct((2 * n_z, 8, LANES), F32),
        ),
        in_specs=[pl.BlockSpec(memory_space=pl.ANY), pl.BlockSpec(memory_space=pltpu.VMEM)],
        out_specs=[pl.BlockSpec(memory_space=pltpu.VMEM)] * 2,
        scratch_shapes=[
            pltpu.VMEM((feats, heads), BF16),
            pltpu.VMEM((heads, half), F32),
            pltpu.VMEM((n_z, 16, half), F32),
            pltpu.VMEM((n_z, 16, half), F32),
            pltpu.VMEM((8, half), F32),
            pltpu.VMEM((8, half), F32),
            dma((n_z, 2)), dma((n_z, 2)), dma, dma, dma((n_z,)), dma((n_z,)), dma, dma, dma((2,)),
        ],
        compiler_params=pltpu.CompilerParams(
            collective_id=0, has_side_effects=True, vmem_limit_bytes=32 * 1024 * 1024
        ),
        cost_estimate=pl.CostEstimate(flops=10**8, bytes_accessed=2 * 10**6, transcendentals=0),
    )(tokens, weight)


def triangles():
    row = lax.broadcasted_iota(jnp.int32, (LANES, LANES), 0)
    col = lax.broadcasted_iota(jnp.int32, (LANES, LANES), 1)
    same = (row < BLK) == (col < BLK)
    upper = jnp.where(row <= col, 1.0, 0.0).astype(F32)
    ahead = jnp.where((row <= col) & same, 1.0, 0.0).astype(F32)
    behind = jnp.where((row >= col) & same, 1.0, 0.0).astype(F32)
    return upper, ahead, behind


def exact_dot(a, b):
    return lax.dot_general(a, b, NN, preferred_element_type=F32, precision=lax.Precision.HIGHEST)


def split_dot(a, b):
    high = b.astype(BF16)
    low = (b - high.astype(F32)).astype(BF16)
    return lax.dot_general(a, high, NT, preferred_element_type=F32) + lax.dot_general(
        a, low, NT, preferred_element_type=F32
    )


def mixer_pair(first, second, pre_ref, starts_ref, rate, bias, gain, x_ref, go_ref, b_ref, c_ref):
    pair = 2 * BLK
    lane = lax.broadcasted_iota(jnp.int32, (8, LANES), 1)
    pre = jnp.where(lane < BLK, pre_ref[first], pltpu.roll(pre_ref[second], BLK, 1))
    starts = jnp.where(lane < BLK, starts_ref[first], pltpu.roll(starts_ref[second], BLK, 1))
    starts = jnp.where(lane < pair, starts, 1.0)
    gate = jnp.where(lane < pair, pre + bias, 0.0)
    e = jnp.exp(-jnp.abs(gate))
    series = e * (1.0 - e * (0.5 - e * (1.0 / 3.0 - e * (0.25 - e * 0.2))))
    log1p = jnp.where(e < 0.02, series, jnp.log(1.0 + e))
    step = jnp.maximum(gate, 0.0) + log1p
    sig = jnp.where(gate >= 0, 1.0, e) / (1.0 + e)
    ratio = jnp.where((gate < 0) & (e < 1e-6), 1.0, sig / jnp.maximum(step, 1e-20))
    upper, ahead, behind = triangles()
    level = exact_dot(jnp.where(lane < pair, -step * rate, 0.0), ahead)
    segment = lax.dot_general(starts.astype(BF16), upper.astype(BF16), NN, preferred_element_type=F32)
    rows = jnp.concatenate([level, step, segment, jnp.zeros((LANES - 24, LANES), F32)], axis=0)
    cols = rows.T
    ii = lax.broadcasted_iota(jnp.int32, (pair, LANES), 0)
    jj = lax.broadcasted_iota(jnp.int32, (pair, LANES), 1)
    same = cols[:pair, 16:17] == segment[0:1]
    away = jnp.where(same & (jj <= ii), 0.0, -1e30)
    away_t = jnp.where(same & (jj >= ii), 0.0, -1e30)

    def both(ref, low, width):
        return jnp.concatenate([ref[first, :, low : low + width], ref[second, :, low : low + width]], axis=0)

    pad = jnp.zeros((LANES - pair, LANES), BF16)
    b = both(b_ref, 0, N)
    c = both(c_ref, 0, N)
    score = lax.dot_general(c, jnp.concatenate([b, pad], axis=0), NT, preferred_element_type=F32)
    score_t = lax.dot_general(b, jnp.concatenate([c, pad], axis=0), NT, preferred_element_type=F32)
    grads, by_value, by_grad = [], [], []
    low_half = jj < 64
    for duo in range(4):
        mix, mix_t = [], []
        for head in (2 * duo, 2 * duo + 1):
            level_col = cols[:pair, head : head + 1]
            step_col = cols[:pair, 8 + head : 9 + head]
            level_row = level[head : head + 1]
            step_row = step[head : head + 1]
            mix.append((score * jnp.exp(level_col - level_row + away) * step_row).astype(BF16))
            mix_t.append((score_t * jnp.exp(level_row - level_col + away_t) * step_col).astype(BF16))
        x = both(x_ref, duo * LANES, LANES)
        go = both(go_ref, duo * LANES, LANES)
        y = lax.dot_general(
            jnp.concatenate(mix, axis=0), jnp.concatenate([x, pad], axis=0), NN, preferred_element_type=F32
        )
        gv = lax.dot_general(
            jnp.concatenate(mix_t, axis=0), jnp.concatenate([go, pad], axis=0), NN, preferred_element_type=F32
        )
        y = jnp.where(low_half, y[:pair], y[pair:])
        gv = jnp.where(low_half, gv[:pair], gv[pair:])
        go = go.astype(F32)
        grads.append((gv + gain[0:1, duo * LANES : (duo + 1) * LANES] * go).astype(BF16))
        by_value.append(x.astype(F32) * gv)
        by_grad.append(go * y)
    zeros = jnp.zeros((LANES - pair, 4 * LANES), F32)
    head_of = lax.broadcasted_iota(jnp.int32, (8, 4 * LANES), 1) // 64
    pick = jnp.where(head_of == lax.broadcasted_iota(jnp.int32, (8, 4 * LANES), 0), 1.0, 0.0).astype(BF16)
    inflow = split_dot(pick, jnp.concatenate([jnp.concatenate(by_value, axis=1), zeros], axis=0))
    outflow = split_dot(pick, jnp.concatenate([jnp.concatenate(by_grad, axis=1), zeros], axis=0))
    grad_log = exact_dot(outflow - inflow, behind)
    grad_pre = inflow * ratio - rate * grad_log * sig
    return grads, grad_pre


def mixer_kernel(
    grid, scale, n_block,
    plan_ref, pre_ref, starts_ref, consts_ref, gain_ref, x_any, go_any, b_any, c_any, xg_ref,
    recv_ref, dw_ref,
    x_ref, go_ref, b_ref, c_ref, comp_ref, send_ref, gps_ref, half_ref, swap_ref, msg_ref, all_ref, heads_ref,
    xt_ref, d_ref, e1_ref, a1_ref, e2_ref, a2_ref, e3_ref,
    load_sem, es_sem, er_sem, ws_sem, wr_sem, gs_sem, gr_sem, cs_sem, cr_sem, xs_sem, xr_sem, ys_sem, yr_sem,
    fs_sem, fr_sem, hs_sem, hr_sem, ks_sem, kr_sem, own_sem,
):
    n_z, n_x, n_y, n_dp = grid.n_z, grid.n_x, grid.n_y, grid.n_dp
    dp, yy, xx, core, yh, z = grid.here()
    shard = yh * n_z + z
    other = (1 - yh) * n_z + z
    across = {"shard": other}

    def at_z(step):
        return {"shard": yh * n_z + (z + step) % n_z}

    def at_x(step):
        return {"dp": grid.dp_of(yy, (xx + step) % n_x, core)}

    def at_y(side, step):
        place = grid.dp_of((yy + step) % n_y, xx, core)
        return {"dp": place, "shard": shard if side == 0 else other}

    sibling = {"dp": grid.dp_of(yy, xx, 1 - core)}

    barrier = pltpu.get_barrier_semaphore()

    @pl.loop(0, n_dp - 1)
    def _(s):
        pl.semaphore_signal(barrier, inc=1, device_id={"dp": grid.partner(s)}, device_id_type=MESH)

    for step in range(1, n_z):
        pl.semaphore_signal(barrier, inc=1, device_id=at_z(step), device_id_type=MESH)
    for step in range(n_y):
        pl.semaphore_signal(barrier, inc=1, device_id=at_y(1, step), device_id_type=MESH)

    group = (shard * 8) // (2 * n_z * 8 // G)
    cols = pl.ds(pl.multiple_of(group * N, N), N)
    loads = [
        pltpu.make_async_copy(x_any, x_ref, load_sem.at[0]),
        pltpu.make_async_copy(go_any, go_ref, load_sem.at[1]),
        pltpu.make_async_copy(b_any.at[:, :, cols], b_ref, load_sem.at[2]),
        pltpu.make_async_copy(c_any.at[:, :, cols], c_ref, load_sem.at[3]),
    ]
    for copy in loads:
        copy.start()
    for copy in loads:
        copy.wait()
    pl.semaphore_wait(barrier, n_dp - 1 + n_z - 1 + n_y)

    def outgoing(s):
        return remote(
            send_ref.at[s], recv_ref.at[s], es_sem.at[s], er_sem.at[s], {"dp": grid.partner(s)}
        )

    rate = consts_ref[0]
    bias = consts_ref[1]
    gain = gain_ref[...]

    @pl.loop(0, n_block // 2)
    def _(k):
        grads, grad_pre = mixer_pair(
            plan_ref[2 * k], plan_ref[2 * k + 1], pre_ref, starts_ref, rate, bias, gain, x_ref, go_ref, b_ref, c_ref
        )
        for duo in range(4):
            comp_ref[2 * k, :, duo * LANES : (duo + 1) * LANES] = grads[duo][:BLK]
            comp_ref[2 * k + 1, :, duo * LANES : (duo + 1) * LANES] = grads[duo][BLK:]
        gps_ref[2 * k] = grad_pre
        gps_ref[2 * k + 1] = pltpu.roll(grad_pre, LANES - BLK, 1)
        for s in (2 * k, 2 * k + 1):
            send_ref[s] = comp_ref[plan_ref[n_block + s]]
            if n_dp > n_block:
                outgoing(s).start()
            else:
                @pl.when(s < n_dp - 1)
                def _():
                    outgoing(s).start()

    for side in range(2):
        half_ref[side] = gather_lanes([gps_ref[plan_ref[n_block + n_dp + side * n_z + i]] for i in range(n_z)])
    swap = remote(half_ref.at[1 - yh], swap_ref, ws_sem, wr_sem, across)
    swap.start()
    if n_dp > n_block:
        @pl.loop(n_block, n_dp)
        def _(s):
            send_ref[s] = comp_ref[plan_ref[n_block + s]]

            @pl.when(s < n_dp - 1)
            def _():
                outgoing(s).start()

    own = pltpu.make_async_copy(send_ref.at[n_dp - 1], recv_ref.at[n_dp - 1], own_sem)
    own.start()
    swap.wait()
    msg_ref[...] = jnp.concatenate([half_ref[yh], swap_ref[...]], axis=0).astype(BF16)
    copies = []
    for step in range(1, n_z):
        copy = remote(msg_ref, all_ref.at[step], gs_sem.at[step], gr_sem.at[step], at_z(step))
        copy.start()
        copies.append(copy)
    for side in range(2):
        xt_ref[side] = xg_ref[side].astype(F32).T.astype(BF16)
    for step in range(n_z):
        if step:
            copies[step - 1].wait()
        message = (all_ref[step] if step else msg_ref[...]).astype(F32)
        place = (z + n_z - step) % n_z
        heads_ref[yh, place] = message[:8]
        heads_ref[1 - yh, place] = message[8:]
    grad_heads = heads_ref[...].reshape(2 * n_z * 8, heads_ref.shape[-1]).astype(BF16)
    unit = dw_ref.shape[0] // n_dp
    piece = n_y * unit
    for side in range(2):
        product = lax.dot_general(xt_ref[side], grad_heads, NT, preferred_element_type=F32)
        for c in range(2):
            for x in range(n_x):
                low = (c * n_x + x) * piece
                d_ref[c, x, side] = product[low : low + piece]
    copy = remote(d_ref.at[1 - core], e1_ref, cs_sem, cr_sem, sibling)
    copy.start()
    copy.wait()
    a1_ref[...] = d_ref[core] + e1_ref[...]
    copies = []
    for step in range(1, n_x):
        copy = remote(a1_ref.at[(xx + step) % n_x], e2_ref.at[step], xs_sem.at[step], xr_sem.at[step], at_x(step))
        copy.start()
        copies.append(copy)
    total = a1_ref[xx]
    for step, copy in enumerate(copies, 1):
        copy.wait()
        total = total + e2_ref[step]
    a2_ref[...] = total
    copies = []
    for side in range(2):
        for step in range(n_y):
            if side or step:
                rows = pl.ds(pl.multiple_of(((yy + step) % n_y) * unit, unit), unit)
                copy = remote(
                    a2_ref.at[side, rows], e3_ref.at[side, step],
                    ys_sem.at[side, step], yr_sem.at[side, step], at_y(side, step),
                )
                copy.start()
                copies.append((side, step, copy))
    total = a2_ref[0, pl.ds(pl.multiple_of(yy * unit, unit), unit)]
    for side, step, copy in copies:
        copy.wait()
        total = total + e3_ref[side, step]
    low = pl.multiple_of((core * n_x + xx) * piece, piece)
    mine = pl.ds(pl.multiple_of(low + yy * unit, unit), unit)
    dw_ref[mine] = total * scale
    copies = []
    for step in range(1, n_y):
        copy = remote(dw_ref.at[mine], dw_ref.at[mine], fs_sem.at[step], fr_sem.at[step], at_y(0, step))
        copy.start()
        copies.append(copy)
    for copy in copies:
        copy.wait()
    mine = pl.ds(low, piece)
    copies = []
    for step in range(1, n_x):
        copy = remote(dw_ref.at[mine], dw_ref.at[mine], hs_sem.at[step], hr_sem.at[step], at_x(step))
        copy.start()
        copies.append(copy)
    for copy in copies:
        copy.wait()
    side_rows = n_x * piece
    mine = pl.ds(pl.multiple_of(core * side_rows, side_rows), side_rows)
    copy = remote(dw_ref.at[mine], dw_ref.at[mine], ks_sem, kr_sem, sibling)
    copy.start()
    copy.wait()

    @pl.loop(0, n_dp - 1)
    def _(s):
        outgoing(s).wait()

    own.wait()


def mix(grid, scale, plan, pre, starts, consts, gain, x, go, b, c, xg):
    n_block, _, width = x.shape
    n_z, n_x, n_y, n_dp = grid.n_z, grid.n_x, grid.n_y, grid.n_dp
    _, half, feats = xg.shape
    heads = 2 * n_z * 8
    unit = feats // n_dp
    piece = n_y * unit
    dma = pltpu.SemaphoreType.DMA
    vmem = pl.BlockSpec(memory_space=pltpu.VMEM)
    hbm = pl.BlockSpec(memory_space=pl.ANY)
    return pl.pallas_call(
        functools.partial(mixer_kernel, grid, scale, n_block),
        out_shape=(
            jax.ShapeDtypeStruct((n_dp, BLK, width), BF16),
            jax.ShapeDtypeStruct((feats, heads), F32),
        ),
        in_specs=[pl.BlockSpec(memory_space=pltpu.SMEM), vmem, vmem, vmem, vmem, hbm, hbm, hbm, hbm, vmem],
        out_specs=[hbm, vmem],
        scratch_shapes=[
            pltpu.VMEM((n_block, BLK, width), BF16),
            pltpu.VMEM((n_block, BLK, width), BF16),
            pltpu.VMEM((n_block, BLK, N), BF16),
            pltpu.VMEM((n_block, BLK, N), BF16),
            pltpu.VMEM((n_block, BLK, width), BF16),
            pltpu.VMEM((n_dp, BLK, width), BF16),
            pltpu.VMEM((n_block, 8, LANES), F32),
            pltpu.VMEM((2, 8, half), F32),
            pltpu.VMEM((8, half), F32),
            pltpu.VMEM((16, half), BF16),
            pltpu.VMEM((n_z, 16, half), BF16),
            pltpu.VMEM((2, n_z, 8, half), F32),
            pltpu.VMEM((2, feats, half), BF16),
            pltpu.VMEM((2, n_x, 2, piece, heads), F32),
            pltpu.VMEM((n_x, 2, piece, heads), F32),
            pltpu.VMEM((n_x, 2, piece, heads), F32),
            pltpu.VMEM((n_x, 2, piece, heads), F32),
            pltpu.VMEM((2, piece, heads), F32),
            pltpu.VMEM((2, n_y, unit, heads), F32),
            dma((4,)), dma((n_dp,)), dma((n_dp,)), dma, dma, dma((n_z,)), dma((n_z,)), dma, dma,
            dma((n_x,)), dma((n_x,)), dma((2, n_y)), dma((2, n_y)), dma((n_y,)), dma((n_y,)),
            dma((n_x,)), dma((n_x,)), dma, dma, dma,
        ],
        compiler_params=pltpu.CompilerParams(
            collective_id=1, has_side_effects=True, vmem_limit_bytes=48 * 1024 * 1024
        ),
        cost_estimate=pl.CostEstimate(flops=10**9, bytes_accessed=10**7, transcendentals=10**6),
    )(plan, pre, starts, consts, gain, x, go, b, c, xg)


def on_device(
    residual_in, conv_out, b_proj, c_proj, grad_out, doc_starts, dest_plan, dt_weight, dt_bias, decay_rate, skip_gain
):
    n_data = lax.axis_size("dp")
    n_shard = lax.axis_size("shard")
    grid = Grid(n_data, n_shard)
    rows = conv_out.shape[0]
    n_block = rows // BLK
    first_head = lax.axis_index("shard") * 8

    slots = jnp.arange(n_data, dtype=jnp.int32)
    blocks = jnp.arange(n_block, dtype=jnp.int32)
    destinations = jnp.arange(n_data, dtype=jnp.int32)
    by_index = jnp.sum(jnp.where(dest_plan[:, None] == destinations[None, :], blocks[:, None] + 1, 0), axis=0)
    arrived = lax.all_to_all(by_index.reshape(n_data, 1), "dp", split_axis=0, concat_axis=0, tiled=True)[:, 0]

    hits = dest_plan[None, :] == grid.partner(slots)[:, None]
    valid = jnp.any(hits, axis=1)
    earlier = jnp.sum(hits[None, :, :] & (slots[None, :, None] < slots[:, None, None]), axis=(1, 2))
    pick = jnp.clip(earlier + valid.astype(jnp.int32) - 1, 0, n_block - 1)
    block_rank = jnp.sum(jnp.where(hits, earlier[:, None], 0), axis=0)
    order = jnp.sum(jnp.where(block_rank[None, :] == blocks[:, None], blocks[None, :], 0), axis=1)
    plan = jnp.concatenate([order, pick, block_rank]).astype(jnp.int32)

    def here(values):
        return lax.dynamic_slice_in_dim(values, first_head, 8, 0)

    consts = jnp.broadcast_to(jnp.stack([here(decay_rate), here(dt_bias)])[:, :, None], (2, 8, LANES))
    gain = jnp.broadcast_to(jnp.repeat(here(skip_gain), 64)[None, :], (8, 512))
    starts = jnp.pad(doc_starts.reshape(n_block, BLK).astype(F32), ((0, 0), (0, LANES - BLK)))
    starts = jnp.broadcast_to(starts[:, None, :], (n_block, 8, LANES))

    xg, pre = project(grid, residual_in, dt_weight)
    scale = float(rows * n_data) ** (-0.5)
    received, dw = mix(
        grid, scale, plan, pre, starts, consts, gain,
        conv_out.reshape(n_block, BLK, -1), grad_out.reshape(n_block, BLK, -1),
        b_proj.reshape(n_block, BLK, -1), c_proj.reshape(n_block, BLK, -1), xg,
    )
    by_slot = arrived[grid.source(slots)]
    sources = jnp.sum(jnp.where(by_slot[None, :] == blocks[:, None] + 1, slots[None, :], 0), axis=1)
    conv_grad = jnp.take(received, sources, axis=0).reshape(rows, -1)
    return conv_grad, dw


def solution(mesh):
    placed = (
        P(("dp", "shard"), None),
        P("dp", "shard"),
        P("dp", None),
        P("dp", None),
        P("dp", "shard"),
        P("dp"),
        P("dp"),
        P("shard", None),
        P(),
        P(),
        P(),
    )
    return jax.shard_map(
        on_device,
        mesh=mesh,
        in_specs=placed,
        out_specs=(P("dp", "shard"), P("shard", None)),
        check_vma=False,
    )
```

```python
import functools

import jax
import jax.numpy as jnp
from jax import lax
from jax.experimental import pallas as pl
from jax.experimental.pallas import tpu as pltpu
from jax.sharding import PartitionSpec as P

N = 128
G = 4
BLK = 48
LANES = 128
MESH = pl.DeviceIdType.MESH
F32 = jnp.float32
BF16 = jnp.bfloat16
NT = (((1,), (1,)), ((), ()))
NN = (((1,), (0,)), ((), ()))
N_YHI = 2
PAIR = 2 * BLK
TILES = 13
FAR = -1e30


class Grid:
    def __init__(self, n_dp, n_shard):
        self.n_dp = n_dp
        self.n_z = n_shard // N_YHI
        self.n_core = 2
        rest = n_dp // 2
        self.n_hb = 2 if rest >= 2 else 1
        rest //= self.n_hb
        self.n_x = min(rest, 4)
        self.n_lb = rest // self.n_x
        self.n_y = self.n_hb * self.n_lb

    def here(self):
        dp = lax.axis_index("dp")
        shard = lax.axis_index("shard")
        core = lax.rem(dp, self.n_core)
        x = lax.rem(dp // self.n_core, self.n_x)
        y = dp // (self.n_core * self.n_x)
        return dp, y, x, core, shard // self.n_z, lax.rem(shard, self.n_z)

    def dp_of(self, y, x, core):
        return (y * self.n_x + x) * self.n_core + core

    def partner(self, s):
        _, y, x, core, _, _ = self.here()
        mc = self.n_core - 1 - s % self.n_core
        mx = self.n_x - 1 - (s // self.n_core) % self.n_x
        t = s // (self.n_core * self.n_x)
        hb = y // self.n_lb
        lb = y % self.n_lb
        hb2 = (hb + self.n_hb - 1 + t // self.n_lb) % self.n_hb
        lb2 = (lb + self.n_lb - 1 + t % self.n_lb) % self.n_lb
        if self.n_lb == 1:
            lb2 = lb
        return self.dp_of(hb2 * self.n_lb + lb2, (x + mx) % self.n_x, (core + mc) % self.n_core)


def remote(src, dst, send, recv, device):
    return pltpu.make_async_remote_copy(
        src_ref=src, dst_ref=dst, send_sem=send, recv_sem=recv, device_id=device, device_id_type=MESH
    )


def lanes():
    return lax.broadcasted_iota(jnp.int32, (8, LANES), 1)


def spread_lanes(whole, low):
    width = whole.shape[1]
    if width % LANES:
        return jnp.pad(whole[:, low : low + PAIR], ((0, 0), (0, LANES - PAIR)))
    tile, off = low // LANES, low % LANES
    first = whole[:, tile * LANES : (tile + 1) * LANES]
    if off == 0:
        return first
    first = pltpu.roll(first, LANES - off, 1)
    if off + PAIR <= LANES:
        return first
    second = pltpu.roll(whole[:, (tile + 1) * LANES : (tile + 2) * LANES], LANES - off, 1)
    return jnp.where(lanes() < LANES - off, first, second)


def gather_lanes(pieces):
    width = len(pieces) * PAIR
    if width % LANES:
        return jnp.concatenate([p[:, :PAIR] for p in pieces], axis=1)
    lane = lanes()
    tiles = [jnp.zeros((8, LANES), F32) for _ in range(width // LANES)]
    for index, piece in enumerate(pieces):
        low = index * PAIR
        tile, off = low // LANES, low % LANES
        moved = pltpu.roll(piece, off, 1) if off else piece
        tiles[tile] = jnp.where((lane >= off) & (lane < off + PAIR), moved, tiles[tile])
        if off + PAIR > LANES:
            tiles[tile + 1] = jnp.where(lane < off + PAIR - LANES, moved, tiles[tile + 1])
    return jnp.concatenate(tiles, axis=1)


def triangle(kind):
    row = lax.broadcasted_iota(jnp.int32, (LANES, LANES), 0)
    col = lax.broadcasted_iota(jnp.int32, (LANES, LANES), 1)
    same = (row < BLK) == (col < BLK)
    if kind == "all":
        keep = row <= col
    elif kind == "ahead":
        keep = (row <= col) & same
    else:
        keep = (row >= col) & same
    return jnp.where(keep, 1.0, 0.0).astype(F32)


def causal(transposed):
    row = lax.broadcasted_iota(jnp.int32, (PAIR, LANES), 0)
    col = lax.broadcasted_iota(jnp.int32, (PAIR, LANES), 1)
    same = ((row < BLK) == (col < BLK)) & (col < PAIR)
    return jnp.where(same & ((row <= col) if transposed else (col <= row)), 0.0, FAR).astype(F32)


def exact_dot(a, b):
    return lax.dot_general(a, b, NN, preferred_element_type=F32, precision=lax.Precision.HIGHEST)


def split_dot(a, b):
    high = b.astype(BF16)
    low = (b - high.astype(F32)).astype(BF16)
    return lax.dot_general(a, high, NT, preferred_element_type=F32) + lax.dot_general(
        a, low, NT, preferred_element_type=F32
    )


def columns_of(*rows):
    filled = LANES - 8 * len(rows)
    return jnp.concatenate(list(rows) + [jnp.zeros((filled, LANES), F32)], axis=0).T


def score_pair(starts, b, c):
    pad = jnp.zeros((LANES - PAIR, N), BF16)
    segment = lax.dot_general(
        starts.astype(BF16), triangle("all").astype(BF16), NN, preferred_element_type=F32
    )
    segment = jnp.where(lanes() < PAIR, segment, -1.0)
    same = columns_of(segment)[:PAIR, 0:1] == segment[0:1]
    score = lax.dot_general(c, jnp.concatenate([b, pad], axis=0), NT, preferred_element_type=F32)
    score_t = lax.dot_general(b, jnp.concatenate([c, pad], axis=0), NT, preferred_element_type=F32)
    return (
        jnp.where(same & (causal(False) == 0.0), score, 0.0),
        jnp.where(same & (causal(True) == 0.0), score_t, 0.0),
    )


def pack_scores(score_t):
    lane = lax.broadcasted_iota(jnp.int32, (16, LANES), 1)

    def packed(first, second, third):
        return jnp.where(lane < 48, first, jnp.where(lane < 96, second, third))

    return (
        packed(score_t[0:16], pltpu.roll(score_t[16:32], 48, 1), pltpu.roll(score_t[32:48], 64, 1)),
        packed(pltpu.roll(score_t[48:64], 80, 1), score_t[64:80], pltpu.roll(score_t[80:96], 16, 1)),
    )


def unpack_scores(one, two):
    return jnp.concatenate(
        [one, pltpu.roll(one, 80, 1), pltpu.roll(one, 64, 1), pltpu.roll(two, 48, 1), two, pltpu.roll(two, 112, 1)],
        axis=0,
    )


def mixer_pair(pre, score, score_t, rate, bias, x_of, go_of):
    lane = lanes()
    gate = jnp.where(lane < PAIR, pre + bias, 0.0)
    e = jnp.exp(-jnp.abs(gate))
    series = e * (1.0 - e * (0.5 - e * (1.0 / 3.0 - e * (0.25 - e * 0.2))))
    log1p = jnp.where(e < 0.02, series, jnp.log(1.0 + e))
    step = jnp.maximum(gate, 0.0) + log1p
    sig = jnp.where(gate >= 0, 1.0, e) / (1.0 + e)
    ratio = jnp.where((gate < 0) & (e < 1e-6), 1.0, sig / jnp.maximum(step, 1e-20))
    level = exact_dot(jnp.where(lane < PAIR, -step * rate, 0.0), triangle("ahead"))
    cols = columns_of(level, step)
    away, away_t = causal(False), causal(True)
    pad = jnp.zeros((LANES - PAIR, LANES), BF16)
    low_half = lax.broadcasted_iota(jnp.int32, (PAIR, LANES), 1) < 64
    by_value, by_grad = [], []
    for duo in range(4):
        mix, mix_t = [], []
        for head in (2 * duo, 2 * duo + 1):
            level_col = cols[:PAIR, head : head + 1]
            step_col = cols[:PAIR, 8 + head : 9 + head]
            level_row = level[head : head + 1]
            step_row = step[head : head + 1]
            mix.append((score * jnp.exp(level_col - level_row + away) * step_row).astype(BF16))
            mix_t.append((score_t * jnp.exp(level_row - level_col + away_t) * step_col).astype(BF16))
        x = x_of(duo)
        go = go_of(duo)
        y = lax.dot_general(
            jnp.concatenate(mix, axis=0), jnp.concatenate([x, pad], axis=0), NN, preferred_element_type=F32
        )
        gv = lax.dot_general(
            jnp.concatenate(mix_t, axis=0), jnp.concatenate([go, pad], axis=0), NN, preferred_element_type=F32
        )
        by_value.append(x.astype(F32) * jnp.where(low_half, gv[:PAIR], gv[PAIR:]))
        by_grad.append(go.astype(F32) * jnp.where(low_half, y[:PAIR], y[PAIR:]))
    zeros = jnp.zeros((LANES - PAIR, 4 * LANES), F32)
    head_of = lax.broadcasted_iota(jnp.int32, (8, 4 * LANES), 1) // 64
    pick = jnp.where(head_of == lax.broadcasted_iota(jnp.int32, (8, 4 * LANES), 0), 1.0, 0.0).astype(BF16)
    inflow = split_dot(pick, jnp.concatenate([jnp.concatenate(by_value, axis=1), zeros], axis=0))
    outflow = split_dot(pick, jnp.concatenate([jnp.concatenate(by_grad, axis=1), zeros], axis=0))
    grad_log = exact_dot(outflow - inflow, triangle("behind"))
    return inflow * ratio - rate * grad_log * sig, level, step


def per_head(ref, first_head):
    row = lax.broadcasted_iota(jnp.int32, (8, LANES), 0)
    out = jnp.zeros((8, LANES), F32)
    for head in range(8):
        out = jnp.where(row == head, ref[first_head + head], out)
    return out


def main_kernel(
    grid, n_block,
    tokens_any, w_ref, x_any, go_any, b_any, c_any, starts_ref, plan_ref, bias_ref, rate_ref,
    got_ref, notes_ref, dw_ref,
    xg_ref, wo_ref, full_ref, part_ref, rs_ref, give_ref, take_ref,
    x_ref, go_ref, b_ref, c_ref, send_ref, pre_ref, segs_ref, score_ref, score_t_ref, tile_ref, level_ref, note_ref,
    gps_ref, half_ref, swap_ref, msg_ref, all_ref, heads_ref, xt_ref, d_ref, e1_ref, a1_ref, e2_ref, a2_ref, e3_ref,
    local_sem, load_sem, vs_sem, vr_sem, ts_sem, tr_sem, ps_sem, pr_sem, ss_sem, sr_sem,
    es_sem, er_sem, ns_sem, nr_sem, ws_sem, wr_sem, gs_sem, gr_sem, cs_sem, cr_sem, xs_sem, xr_sem, ys_sem, yr_sem,
    fs_sem, fr_sem, hs_sem, hr_sem, ks_sem, kr_sem, own_sem,
):
    n_z, n_x, n_y, n_dp = grid.n_z, grid.n_x, grid.n_y, grid.n_dp
    dp, yy, xx, core, yh, z = grid.here()
    shard = yh * n_z + z
    other = (1 - yh) * n_z + z
    across = {"shard": other}
    sibling = {"dp": grid.dp_of(yy, xx, 1 - core)}
    feats = w_ref.shape[0]
    per_half = n_z // 2

    def at_z(step):
        return {"shard": yh * n_z + (z + step) % n_z}

    def at_x(step):
        return {"dp": grid.dp_of(yy, (xx + step) % n_x, core)}

    def at_y(side, step):
        place = grid.dp_of((yy + step) % n_y, xx, core)
        return {"dp": place, "shard": shard if side == 0 else other}

    barrier = pltpu.get_barrier_semaphore()
    for step in range(1, n_z):
        pl.semaphore_signal(barrier, inc=1, device_id=at_z(step), device_id_type=MESH)
    for step in range(n_y):
        pl.semaphore_signal(barrier, inc=1, device_id=at_y(1, step), device_id_type=MESH)

    @pl.loop(0, n_dp - 1)
    def _(s):
        pl.semaphore_signal(barrier, inc=1, device_id={"dp": grid.partner(s)}, device_id_type=MESH)

    def feature_columns(side, step):
        owner = (yh if side == 0 else 1 - yh) * n_z + (z + step) % n_z
        return tokens_any.at[:, pl.ds(pl.multiple_of(owner * feats, feats), feats)]

    mine = pl.ds(pl.multiple_of(z * BLK, BLK), BLK)
    group = (shard * 8) // (2 * n_z * 8 // G)
    cols = pl.ds(pl.multiple_of(group * N, N), N)
    loads = [
        pltpu.make_async_copy(b_any.at[:, :, cols], b_ref, load_sem.at[2]),
        pltpu.make_async_copy(c_any.at[:, :, cols], c_ref, load_sem.at[3]),
        pltpu.make_async_copy(go_any, go_ref, load_sem.at[1]),
        pltpu.make_async_copy(x_any, x_ref, load_sem.at[0]),
    ]
    for side in range(2):
        loads.append(pltpu.make_async_copy(feature_columns(side, 0), xg_ref.at[side, mine], local_sem.at[side]))
    for copy in loads:
        copy.start()
    pl.semaphore_wait(barrier, n_dp - 1 + n_z - 1 + n_y)

    weight_swap = remote(w_ref, wo_ref, vs_sem, vr_sem, across)
    weight_swap.start()
    token_copies = []
    for step in range(1, n_z):
        for side in range(2):
            copy = remote(
                feature_columns(side, step), xg_ref.at[side, mine],
                ts_sem.at[step, side], tr_sem.at[step, side], at_z(step),
            )
            copy.start()
            token_copies.append(copy)

    for copy in loads[:3]:
        copy.wait()
    marks = jnp.broadcast_to(starts_ref[...].astype(F32), (8, n_block * BLK))
    for q in range(n_block // 2):
        segs_ref[q] = spread_lanes(marks, q * PAIR)

    def both(ref, q, low):
        return jnp.concatenate([ref[2 * q, :, pl.ds(low, LANES)], ref[2 * q + 1, :, pl.ds(low, LANES)]], axis=0)

    @pl.loop(0, n_block // 2)
    def _(q):
        score, score_t = score_pair(segs_ref[q], both(b_ref, q, 0), both(c_ref, q, 0))
        score_ref[q] = score
        score_t_ref[q] = score_t
        one, two = pack_scores(score_t)
        tile_ref[2 * q] = one.astype(BF16)
        tile_ref[2 * q + 1] = two.astype(BF16)

    def label_of(s):
        target = grid.partner(s)
        label = jnp.int32(0)
        for block in range(n_block):
            label = label + jnp.where(plan_ref[block] == target, block + 1, 0)
        return label

    def outgoing(s):
        return remote(send_ref.at[s], got_ref.at[s], es_sem.at[s], er_sem.at[s], {"dp": grid.partner(s)})

    def noted(s):
        return remote(note_ref.at[s], notes_ref.at[s], ns_sem.at[s], nr_sem.at[s], {"dp": grid.partner(s)})

    @pl.loop(0, n_dp)
    def _(s):
        block = jnp.clip(label_of(s) - 1, 0, n_block - 1)
        whole = go_ref[block]
        for r in range(3):
            for t in range(4):
                send_ref[s, 4 * r + t] = whole[16 * r : 16 * r + 16, t * LANES : (t + 1) * LANES]
        send_ref[s, TILES - 1] = tile_ref[block]

        @pl.when(s < n_dp - 1)
        def _():
            outgoing(s).start()

    own = pltpu.make_async_copy(send_ref.at[n_dp - 1], got_ref.at[n_dp - 1], own_sem.at[0])
    own.start()

    w_here = w_ref[...].astype(F32).T.astype(BF16)
    for copy in loads[3:]:
        copy.wait()
    weight_swap.wait()
    w_other = wo_ref[...].astype(F32).T.astype(BF16)
    for copy in token_copies:
        copy.wait()
    full_ref[...] = lax.dot_general(w_here, xg_ref[0], NT, preferred_element_type=F32) + lax.dot_general(
        w_other, xg_ref[1], NT, preferred_element_type=F32
    )
    copies = []
    for step in list(range(1, n_z)) + [0]:
        for side in range(2):
            owner = (yh if side == 0 else 1 - yh) * n_z + (z + step) % n_z
            part_ref[step, side * 8 : (side + 1) * 8] = full_ref[pl.ds(pl.multiple_of(owner * 8, 8), 8)]
        if step:
            copy = remote(part_ref.at[step], rs_ref.at[step], ps_sem.at[step], pr_sem.at[step], at_z(step))
            copy.start()
            copies.append(copy)
    for side in range(2):
        xt_ref[side] = xg_ref[side].astype(F32).T.astype(BF16)
    total = part_ref[0]
    for step, copy in enumerate(copies, 1):
        copy.wait()
        total = total + rs_ref[step]
    give_ref[...] = total[8:]
    logit_swap = remote(give_ref, take_ref, ss_sem, sr_sem, across)
    logit_swap.start()
    for q in range(per_half):
        pre_ref[yh * per_half + q] = spread_lanes(total[:8], q * PAIR)

    rate = per_head(rate_ref, shard * 8)
    bias = per_head(bias_ref, shard * 8)
    lane = lanes()

    def work(q):
        grad_pre, level, step = mixer_pair(
            pre_ref[q], score_ref[q], score_t_ref[q], rate, bias,
            lambda duo: both(x_ref, q, duo * LANES), lambda duo: both(go_ref, q, duo * LANES),
        )
        gps_ref[q] = grad_pre
        level_ref[2 * q] = jnp.where(lane < BLK, level, pltpu.roll(step, BLK, 1))
        level_ref[2 * q + 1] = jnp.where(lane < BLK, pltpu.roll(level, LANES - BLK, 1), step)

    @pl.loop(0, per_half // 2)
    def _(q):
        work(yh * per_half + q)

    logit_swap.wait()
    others = take_ref[...]
    for q in range(per_half):
        pre_ref[(1 - yh) * per_half + q] = spread_lanes(others, q * PAIR)

    @pl.loop(0, per_half)
    def _(q):
        work((1 - yh) * per_half + q)

    half_ref[0] = gather_lanes([gps_ref[(1 - yh) * per_half + i] for i in range(per_half)])
    grad_swap = remote(half_ref.at[0], swap_ref, ws_sem, wr_sem, across)
    grad_swap.start()

    @pl.loop(per_half // 2, per_half)
    def _(q):
        work(yh * per_half + q)

    mine_half = gather_lanes([gps_ref[yh * per_half + i] for i in range(per_half)])
    grad_swap.wait()
    msg_ref[...] = jnp.concatenate([mine_half, swap_ref[...]], axis=0).astype(BF16)
    copies = []
    for step in range(1, n_z):
        copy = remote(msg_ref, all_ref.at[step], gs_sem.at[step], gr_sem.at[step], at_z(step))
        copy.start()
        copies.append(copy)

    @pl.loop(0, n_dp)
    def _(s):
        label = label_of(s)
        note_ref[s] = jnp.where(lane < PAIR, level_ref[jnp.clip(label - 1, 0, n_block - 1)], label.astype(F32))

        @pl.when(s < n_dp - 1)
        def _():
            noted(s).start()

    own_note = pltpu.make_async_copy(note_ref.at[n_dp - 1], notes_ref.at[n_dp - 1], own_sem.at[1])
    own_note.start()

    for step in range(n_z):
        if step:
            copies[step - 1].wait()
        message = (all_ref[step] if step else msg_ref[...]).astype(F32)
        place = (z + n_z - step) % n_z
        heads_ref[yh, place] = message[:8]
        heads_ref[1 - yh, place] = message[8:]
    grad_heads = heads_ref[...].reshape(2 * n_z * 8, heads_ref.shape[-1]).astype(BF16)
    unit = dw_ref.shape[0] // n_dp
    piece = n_y * unit
    for side in range(2):
        product = lax.dot_general(xt_ref[side], grad_heads, NT, preferred_element_type=F32)
        for c in range(2):
            for x in range(n_x):
                low = (c * n_x + x) * piece
                d_ref[c, x, side] = product[low : low + piece]
    copy = remote(d_ref.at[1 - core], e1_ref, cs_sem, cr_sem, sibling)
    copy.start()
    copy.wait()
    a1_ref[...] = d_ref[core] + e1_ref[...]
    copies = []
    for step in range(1, n_x):
        copy = remote(a1_ref.at[(xx + step) % n_x], e2_ref.at[step], xs_sem.at[step], xr_sem.at[step], at_x(step))
        copy.start()
        copies.append(copy)
    total = a1_ref[xx]
    for step, copy in enumerate(copies, 1):
        copy.wait()
        total = total + e2_ref[step]
    a2_ref[...] = total
    copies = []
    for side in range(2):
        for step in range(n_y):
            if side or step:
                rows = pl.ds(pl.multiple_of(((yy + step) % n_y) * unit, unit), unit)
                copy = remote(
                    a2_ref.at[side, rows], e3_ref.at[side, step],
                    ys_sem.at[side, step], yr_sem.at[side, step], at_y(side, step),
                )
                copy.start()
                copies.append((side, step, copy))
    total = a2_ref[0, pl.ds(pl.multiple_of(yy * unit, unit), unit)]
    for side, step, copy in copies:
        copy.wait()
        total = total + e3_ref[side, step]
    low = pl.multiple_of((core * n_x + xx) * piece, piece)
    mine = pl.ds(pl.multiple_of(low + yy * unit, unit), unit)
    dw_ref[mine] = total * (float(n_dp * n_block * BLK) ** -0.5)
    copies = []
    for step in range(1, n_y):
        copy = remote(dw_ref.at[mine], dw_ref.at[mine], fs_sem.at[step], fr_sem.at[step], at_y(0, step))
        copy.start()
        copies.append(copy)
    for copy in copies:
        copy.wait()
    mine = pl.ds(low, piece)
    copies = []
    for step in range(1, n_x):
        copy = remote(dw_ref.at[mine], dw_ref.at[mine], hs_sem.at[step], hr_sem.at[step], at_x(step))
        copy.start()
        copies.append(copy)
    for copy in copies:
        copy.wait()
    side_rows = n_x * piece
    mine = pl.ds(pl.multiple_of(core * side_rows, side_rows), side_rows)
    copy = remote(dw_ref.at[mine], dw_ref.at[mine], ks_sem, kr_sem, sibling)
    copy.start()
    copy.wait()

    @pl.loop(0, n_dp - 1)
    def _(s):
        noted(s).wait()
        outgoing(s).wait()

    own.wait()
    own_note.wait()


def main_call(grid, tokens, weight, x, go, b, c, starts, plan, bias, rate):
    n_block, _, width = x.shape
    n_z, n_x, n_y, n_dp = grid.n_z, grid.n_x, grid.n_y, grid.n_dp
    half = n_z * BLK
    feats, heads = weight.shape
    unit = feats // n_dp
    piece = n_y * unit
    n_pair = n_block // 2
    dma = pltpu.SemaphoreType.DMA
    vmem = pl.BlockSpec(memory_space=pltpu.VMEM)
    smem = pl.BlockSpec(memory_space=pltpu.SMEM)
    hbm = pl.BlockSpec(memory_space=pl.ANY)
    return pl.pallas_call(
        functools.partial(main_kernel, grid, n_block),
        out_shape=(
            jax.ShapeDtypeStruct((n_dp, TILES, 16, LANES), BF16),
            jax.ShapeDtypeStruct((n_dp, 8, LANES), F32),
            jax.ShapeDtypeStruct((feats, heads), F32),
        ),
        in_specs=[hbm, vmem, hbm, hbm, hbm, hbm, vmem, smem, smem, smem],
        out_specs=[hbm, hbm, vmem],
        scratch_shapes=[
            pltpu.VMEM((2, half, feats), BF16),
            pltpu.VMEM((feats, heads), BF16),
            pltpu.VMEM((heads, half), F32),
            pltpu.VMEM((n_z, 16, half), F32),
            pltpu.VMEM((n_z, 16, half), F32),
            pltpu.VMEM((8, half), F32),
            pltpu.VMEM((8, half), F32),
            pltpu.VMEM((n_block, BLK, width), BF16),
            pltpu.VMEM((n_block, BLK, width), BF16),
            pltpu.VMEM((n_block, BLK, N), BF16),
            pltpu.VMEM((n_block, BLK, N), BF16),
            pltpu.VMEM((n_dp, TILES, 16, LANES), BF16),
            pltpu.VMEM((n_pair, 8, LANES), F32),
            pltpu.VMEM((n_pair, 8, LANES), F32),
            pltpu.VMEM((n_pair, PAIR, LANES), F32),
            pltpu.VMEM((n_pair, PAIR, LANES), F32),
            pltpu.VMEM((n_block, 16, LANES), BF16),
            pltpu.VMEM((n_block, 8, LANES), F32),
            pltpu.VMEM((n_dp, 8, LANES), F32),
            pltpu.VMEM((n_pair, 8, LANES), F32),
            pltpu.VMEM((1, 8, half), F32),
            pltpu.VMEM((8, half), F32),
            pltpu.VMEM((16, half), BF16),
            pltpu.VMEM((n_z, 16, half), BF16),
            pltpu.VMEM((2, n_z, 8, half), F32),
            pltpu.VMEM((2, feats, half), BF16),
            pltpu.VMEM((2, n_x, 2, piece, heads), F32),
            pltpu.VMEM((n_x, 2, piece, heads), F32),
            pltpu.VMEM((n_x, 2, piece, heads), F32),
            pltpu.VMEM((n_x, 2, piece, heads), F32),
            pltpu.VMEM((2, piece, heads), F32),
            pltpu.VMEM((2, n_y, unit, heads), F32),
            dma((2,)), dma((4,)), dma, dma, dma((n_z, 2)), dma((n_z, 2)), dma((n_z,)), dma((n_z,)), dma, dma,
            dma((n_dp,)), dma((n_dp,)), dma((n_dp,)), dma((n_dp,)), dma, dma, dma((n_z,)), dma((n_z,)), dma, dma,
            dma((n_x,)), dma((n_x,)), dma((2, n_y)), dma((2, n_y)), dma((n_y,)), dma((n_y,)),
            dma((n_x,)), dma((n_x,)), dma, dma, dma((2,)),
        ],
        compiler_params=pltpu.CompilerParams(
            collective_id=0, has_side_effects=True, vmem_limit_bytes=60 * 1024 * 1024
        ),
        cost_estimate=pl.CostEstimate(flops=10**9, bytes_accessed=10**7, transcendentals=10**6),
    )(tokens, weight, x, go, b, c, starts, plan, bias, rate)


def finish_kernel(source_ref, gain_ref, got_ref, note_ref, dw_in_ref, out_ref, dw_ref):
    shard = lax.axis_index("shard")
    lane = lanes()
    dw_ref[...] = dw_in_ref[...]
    away_t = causal(True)
    pad = jnp.zeros((LANES - PAIR, LANES), BF16)
    low_half = lax.broadcasted_iota(jnp.int32, (PAIR, LANES), 1) < 64

    @pl.loop(0, out_ref.shape[0] // 2)
    def _(q):
        last = got_ref.shape[0] - 1
        first = jnp.clip(source_ref[2 * q], 0, last)
        second = jnp.clip(source_ref[2 * q + 1], 0, last)
        one, two = note_ref[first], note_ref[second]
        level = jnp.where(lane < BLK, one, jnp.where(lane < PAIR, pltpu.roll(two, BLK, 1), 0.0))
        step = jnp.where(lane < BLK, pltpu.roll(one, LANES - BLK, 1), jnp.where(lane < PAIR, two, 0.0))
        cols = columns_of(level, step)
        score_t = unpack_scores(
            got_ref[first, TILES - 1].astype(F32), got_ref[second, TILES - 1].astype(F32)
        )
        for duo in range(4):
            mix_t = []
            for head in (2 * duo, 2 * duo + 1):
                level_col = cols[:PAIR, head : head + 1]
                step_col = cols[:PAIR, 8 + head : 9 + head]
                mix_t.append(
                    (score_t * jnp.exp(level[head : head + 1] - level_col + away_t) * step_col).astype(BF16)
                )
            go = jnp.concatenate(
                [got_ref[first, 4 * r + duo] for r in range(3)] + [got_ref[second, 4 * r + duo] for r in range(3)],
                axis=0,
            )
            gv = lax.dot_general(
                jnp.concatenate(mix_t, axis=0), jnp.concatenate([go, pad], axis=0), NN, preferred_element_type=F32
            )
            gv = jnp.where(low_half, gv[:PAIR], gv[PAIR:])
            gain = jnp.where(low_half, gain_ref[shard * 8 + 2 * duo], gain_ref[shard * 8 + 2 * duo + 1])
            grad = (gv + gain * go.astype(F32)).astype(BF16)
            out_ref[2 * q, :, duo * LANES : (duo + 1) * LANES] = grad[:BLK]
            out_ref[2 * q + 1, :, duo * LANES : (duo + 1) * LANES] = grad[BLK:]


def finish(sources, gain, got, notes, dw, n_block):
    vmem = pl.BlockSpec(memory_space=pltpu.VMEM)
    smem = pl.BlockSpec(memory_space=pltpu.SMEM)
    return pl.pallas_call(
        finish_kernel,
        out_shape=(
            jax.ShapeDtypeStruct((n_block, BLK, 4 * LANES), BF16),
            jax.ShapeDtypeStruct(dw.shape, F32),
        ),
        in_specs=[smem, smem, vmem, vmem, vmem],
        out_specs=[vmem, vmem],
        compiler_params=pltpu.CompilerParams(vmem_limit_bytes=60 * 1024 * 1024),
        cost_estimate=pl.CostEstimate(flops=10**8, bytes_accessed=4 * 10**6, transcendentals=10**6),
    )(sources, gain, got, notes, dw)


def on_device(
    residual_in, conv_out, b_proj, c_proj, grad_out, doc_starts, dest_plan, dt_weight, dt_bias, decay_rate, skip_gain
):
    n_data = lax.axis_size("dp")
    grid = Grid(n_data, lax.axis_size("shard"))
    rows = conv_out.shape[0]
    n_block = rows // BLK

    def blocked(values):
        return values.reshape(n_block, BLK, -1)

    got, notes, dw = main_call(
        grid, residual_in, dt_weight, blocked(conv_out), blocked(grad_out), blocked(b_proj), blocked(c_proj),
        doc_starts.reshape(1, rows), dest_plan, dt_bias, decay_rate,
    )
    labels = notes[:, 0, LANES - 1].astype(jnp.int32)
    slots = jnp.arange(n_data, dtype=jnp.int32)
    wanted = jnp.arange(1, n_block + 1, dtype=jnp.int32)
    sources = jnp.sum(jnp.where(labels[None, :] == wanted[:, None], slots[None, :], 0), axis=1)
    conv_grad, dw = finish(sources, skip_gain, got, notes, dw, n_block)
    return conv_grad.reshape(rows, -1), dw


def solution(mesh):
    placed = (
        P(("dp", "shard"), None),
        P("dp", "shard"),
        P("dp", None),
        P("dp", None),
        P("dp", "shard"),
        P("dp"),
        P("dp"),
        P("shard", None),
        P(),
        P(),
        P(),
    )
    return jax.shard_map(
        on_device,
        mesh=mesh,
        in_specs=placed,
        out_specs=(P("dp", "shard"), P("shard", None)),
        check_vma=False,
    )
```

```python
import functools
import math

import jax
import jax.numpy as jnp
from jax import lax
from jax.experimental import pallas as pl
from jax.experimental.pallas import tpu as pltpu
from jax.sharding import PartitionSpec as P

N = 128
G = 4
BLK = 48
LANES = 128
MESH = pl.DeviceIdType.MESH
F32 = jnp.float32
BF16 = jnp.bfloat16
NT = (((1,), (1,)), ((), ()))
NN = (((1,), (0,)), ((), ()))
N_YHI = 2
PAIR = 2 * BLK
TILES = 13
FAR = -1e30
FAR_ENDS = (6, 8, 14, 16)
NEAR_ENDS = (6, 8, 12, 15)


class Grid:
    def __init__(self, n_dp, n_shard):
        self.n_dp = n_dp
        self.n_z = n_shard // N_YHI
        self.n_core = 2
        rest = n_dp // 2
        self.n_hb = 2 if rest >= 2 else 1
        rest //= self.n_hb
        self.n_x = min(rest, 4)
        self.n_lb = rest // self.n_x
        self.n_y = self.n_hb * self.n_lb

    def here(self):
        dp = lax.axis_index("dp")
        shard = lax.axis_index("shard")
        core = lax.rem(dp, self.n_core)
        x = lax.rem(dp // self.n_core, self.n_x)
        y = dp // (self.n_core * self.n_x)
        return dp, y, x, core, shard // self.n_z, lax.rem(shard, self.n_z)

    def dp_of(self, y, x, core):
        return (y * self.n_x + x) * self.n_core + core

    def partner(self, s):
        _, y, x, core, _, _ = self.here()
        mc = self.n_core - 1 - s % self.n_core
        mx = self.n_x - 1 - (s // self.n_core) % self.n_x
        t = s // (self.n_core * self.n_x)
        hb = y // self.n_lb
        lb = y % self.n_lb
        hb2 = (hb + self.n_hb - 1 + t // self.n_lb) % self.n_hb
        lb2 = (lb + self.n_lb - 1 + t % self.n_lb) % self.n_lb
        if self.n_lb == 1:
            lb2 = lb
        return self.dp_of(hb2 * self.n_lb + lb2, (x + mx) % self.n_x, (core + mc) % self.n_core)


def remote(src, dst, send, recv, device):
    return pltpu.make_async_remote_copy(
        src_ref=src, dst_ref=dst, send_sem=send, recv_sem=recv, device_id=device, device_id_type=MESH
    )


def lanes():
    return lax.broadcasted_iota(jnp.int32, (8, LANES), 1)


def spread_lanes(whole, low):
    width = whole.shape[1]
    if width % LANES:
        return jnp.pad(whole[:, low : low + PAIR], ((0, 0), (0, LANES - PAIR)))
    tile, off = low // LANES, low % LANES
    first = whole[:, tile * LANES : (tile + 1) * LANES]
    if off == 0:
        return first
    first = pltpu.roll(first, LANES - off, 1)
    if off + PAIR <= LANES:
        return first
    second = pltpu.roll(whole[:, (tile + 1) * LANES : (tile + 2) * LANES], LANES - off, 1)
    return jnp.where(lanes() < LANES - off, first, second)


def gather_lanes(pieces):
    width = len(pieces) * PAIR
    if width % LANES:
        return jnp.concatenate([p[:, :PAIR] for p in pieces], axis=1)
    lane = lanes()
    tiles = [jnp.zeros((8, LANES), F32) for _ in range(width // LANES)]
    for index, piece in enumerate(pieces):
        low = index * PAIR
        tile, off = low // LANES, low % LANES
        moved = pltpu.roll(piece, off, 1) if off else piece
        tiles[tile] = jnp.where((lane >= off) & (lane < off + PAIR), moved, tiles[tile])
        if off + PAIR > LANES:
            tiles[tile + 1] = jnp.where(lane < off + PAIR - LANES, moved, tiles[tile + 1])
    return jnp.concatenate(tiles, axis=1)


def triangle(kind):
    row = lax.broadcasted_iota(jnp.int32, (LANES, LANES), 0)
    col = lax.broadcasted_iota(jnp.int32, (LANES, LANES), 1)
    same = (row < BLK) == (col < BLK)
    if kind == "all":
        keep = row <= col
    elif kind == "ahead":
        keep = (row <= col) & same
    else:
        keep = (row >= col) & same
    return jnp.where(keep, 1.0, 0.0).astype(F32)


def causal(transposed):
    row = lax.broadcasted_iota(jnp.int32, (PAIR, LANES), 0)
    col = lax.broadcasted_iota(jnp.int32, (PAIR, LANES), 1)
    same = ((row < BLK) == (col < BLK)) & (col < PAIR)
    return jnp.where(same & ((row <= col) if transposed else (col <= row)), 0.0, FAR).astype(F32)


def exact_dot(a, b):
    return lax.dot_general(a, b, NN, preferred_element_type=F32, precision=lax.Precision.HIGHEST)


def split_dot(a, b):
    high = b.astype(BF16)
    low = (b - high.astype(F32)).astype(BF16)
    return lax.dot_general(a, high, NT, preferred_element_type=F32) + lax.dot_general(
        a, low, NT, preferred_element_type=F32
    )


def columns_of(*rows):
    filled = LANES - 8 * len(rows)
    return jnp.concatenate(list(rows) + [jnp.zeros((filled, LANES), F32)], axis=0).T


def score_pair(starts, b, c):
    pad = jnp.zeros((LANES - PAIR, N), BF16)
    segment = lax.dot_general(
        starts.astype(BF16), triangle("all").astype(BF16), NN, preferred_element_type=F32
    )
    segment = jnp.where(lanes() < PAIR, segment, -1.0)
    same = columns_of(segment)[:PAIR, 0:1] == segment[0:1]
    score = lax.dot_general(c, jnp.concatenate([b, pad], axis=0), NT, preferred_element_type=F32)
    score_t = lax.dot_general(b, jnp.concatenate([c, pad], axis=0), NT, preferred_element_type=F32)
    return (
        jnp.where(same & (causal(False) == 0.0), score, 0.0),
        jnp.where(same & (causal(True) == 0.0), score_t, 0.0),
    )


def pack_scores(score_t):
    lane = lax.broadcasted_iota(jnp.int32, (16, LANES), 1)

    def packed(first, second, third):
        return jnp.where(lane < 48, first, jnp.where(lane < 96, second, third))

    return (
        packed(score_t[0:16], pltpu.roll(score_t[16:32], 48, 1), pltpu.roll(score_t[32:48], 64, 1)),
        packed(pltpu.roll(score_t[48:64], 80, 1), score_t[64:80], pltpu.roll(score_t[80:96], 16, 1)),
    )


def unpack_scores(one, two):
    return jnp.concatenate(
        [one, pltpu.roll(one, 80, 1), pltpu.roll(one, 64, 1), pltpu.roll(two, 48, 1), two, pltpu.roll(two, 112, 1)],
        axis=0,
    )


def mixer_pair(pre, score, score_t, rate, bias, x_of, go_of):
    lane = lanes()
    gate = jnp.where(lane < PAIR, pre + bias, 0.0)
    e = jnp.exp(-jnp.abs(gate))
    series = e * (1.0 - e * (0.5 - e * (1.0 / 3.0 - e * (0.25 - e * 0.2))))
    log1p = jnp.where(e < 0.02, series, jnp.log(1.0 + e))
    step = jnp.maximum(gate, 0.0) + log1p
    sig = jnp.where(gate >= 0, 1.0, e) / (1.0 + e)
    ratio = jnp.where((gate < 0) & (e < 1e-6), 1.0, sig / jnp.maximum(step, 1e-20))
    level = exact_dot(jnp.where(lane < PAIR, -step * rate, 0.0), triangle("ahead"))
    cols = columns_of(level, step)
    away, away_t = causal(False), causal(True)
    pad = jnp.zeros((LANES - PAIR, LANES), BF16)
    low_half = lax.broadcasted_iota(jnp.int32, (PAIR, LANES), 1) < 64
    by_value, by_grad = [], []
    for duo in range(4):
        mix, mix_t = [], []
        for head in (2 * duo, 2 * duo + 1):
            level_col = cols[:PAIR, head : head + 1]
            step_col = cols[:PAIR, 8 + head : 9 + head]
            level_row = level[head : head + 1]
            step_row = step[head : head + 1]
            mix.append((score * jnp.exp(level_col - level_row + away) * step_row).astype(BF16))
            mix_t.append((score_t * jnp.exp(level_row - level_col + away_t) * step_col).astype(BF16))
        x = x_of(duo)
        go = go_of(duo)
        y = lax.dot_general(
            jnp.concatenate(mix, axis=0), jnp.concatenate([x, pad], axis=0), NN, preferred_element_type=F32
        )
        gv = lax.dot_general(
            jnp.concatenate(mix_t, axis=0), jnp.concatenate([go, pad], axis=0), NN, preferred_element_type=F32
        )
        by_value.append(x.astype(F32) * jnp.where(low_half, gv[:PAIR], gv[PAIR:]))
        by_grad.append(go.astype(F32) * jnp.where(low_half, y[:PAIR], y[PAIR:]))
    zeros = jnp.zeros((LANES - PAIR, 4 * LANES), F32)
    head_of = lax.broadcasted_iota(jnp.int32, (8, 4 * LANES), 1) // 64
    pick = jnp.where(head_of == lax.broadcasted_iota(jnp.int32, (8, 4 * LANES), 0), 1.0, 0.0).astype(BF16)
    inflow = split_dot(pick, jnp.concatenate([jnp.concatenate(by_value, axis=1), zeros], axis=0))
    outflow = split_dot(pick, jnp.concatenate([jnp.concatenate(by_grad, axis=1), zeros], axis=0))
    grad_log = exact_dot(outflow - inflow, triangle("behind"))
    return inflow * ratio - rate * grad_log * sig, level, step


def per_head(ref, first_head):
    row = lax.broadcasted_iota(jnp.int32, (8, LANES), 0)
    out = jnp.zeros((8, LANES), F32)
    for head in range(8):
        out = jnp.where(row == head, ref[first_head + head], out)
    return out


def main_kernel(
    grid, n_block,
    tokens_any, w_ref, x_any, go_any, b_any, c_any, starts_ref, plan_ref, bias_ref, rate_ref,
    got_ref, notes_ref, dw_ref,
    xg_ref, wo_ref, full_ref, part_ref, rs_ref, give_ref, take_ref,
    x_ref, go_ref, b_ref, c_ref, send_ref, pre_ref, segs_ref, score_ref, score_t_ref, tile_ref, level_ref, note_ref,
    gps_ref, half_ref, swap_ref, msg_ref, all_ref, heads_ref, xt_ref, d_ref, e1_ref, a1_ref, e2_ref,
    local_sem, load_sem, vs_sem, vr_sem, ts_sem, tr_sem, ps_sem, pr_sem, ss_sem, sr_sem,
    es_sem, er_sem, ns_sem, nr_sem, ws_sem, wr_sem, gs_sem, gr_sem, cs_sem, cr_sem, xs_sem, xr_sem,
    hs_sem, hr_sem, ks_sem, kr_sem, own_sem,
):
    n_z, n_x, n_y, n_dp = grid.n_z, grid.n_x, grid.n_y, grid.n_dp
    dp, yy, xx, core, yh, z = grid.here()
    shard = yh * n_z + z
    other = (1 - yh) * n_z + z
    across = {"shard": other}
    sibling = {"dp": grid.dp_of(yy, xx, 1 - core)}
    feats = w_ref.shape[0]
    per_half = n_z // 2

    def at_z(step):
        return {"shard": yh * n_z + (z + step) % n_z}

    def at_xy(side, step_x, step_y):
        place = grid.dp_of((yy + step_y) % n_y, (xx + step_x) % n_x, core)
        return {"dp": place, "shard": shard if side == 0 else other}

    plane = [(step_x, step_y) for step_x in range(n_x) for step_y in range(n_y)]

    barrier = pltpu.get_barrier_semaphore()
    for step in range(1, n_z):
        pl.semaphore_signal(barrier, inc=1, device_id=at_z(step), device_id_type=MESH)
    for step_x, step_y in plane:
        pl.semaphore_signal(barrier, inc=1, device_id=at_xy(1, step_x, step_y), device_id_type=MESH)

    @pl.loop(0, n_dp - 1)
    def _(s):
        pl.semaphore_signal(barrier, inc=1, device_id={"dp": grid.partner(s)}, device_id_type=MESH)

    def feature_columns(side, step):
        owner = (yh if side == 0 else 1 - yh) * n_z + (z + step) % n_z
        return tokens_any.at[:, pl.ds(pl.multiple_of(owner * feats, feats), feats)]

    mine = pl.ds(pl.multiple_of(z * BLK, BLK), BLK)
    group = (shard * 8) // (2 * n_z * 8 // G)
    cols = pl.ds(pl.multiple_of(group * N, N), N)
    loads = [
        pltpu.make_async_copy(b_any.at[:, :, cols], b_ref, load_sem.at[2]),
        pltpu.make_async_copy(c_any.at[:, :, cols], c_ref, load_sem.at[3]),
        pltpu.make_async_copy(go_any, go_ref, load_sem.at[1]),
        pltpu.make_async_copy(x_any, x_ref, load_sem.at[0]),
    ]
    for side in range(2):
        loads.append(pltpu.make_async_copy(feature_columns(side, 0), xg_ref.at[side, mine], local_sem.at[side]))
    for copy in loads:
        copy.start()
    pl.semaphore_wait(barrier, n_dp - 1 + n_z - 1 + n_x * n_y)

    weight_swap = remote(w_ref, wo_ref, vs_sem, vr_sem, across)
    weight_swap.start()
    token_copies = []
    for step in range(1, n_z):
        for side in range(2):
            copy = remote(
                feature_columns(side, step), xg_ref.at[side, mine],
                ts_sem.at[step, side], tr_sem.at[step, side], at_z(step),
            )
            copy.start()
            token_copies.append(copy)

    for copy in loads[:3]:
        copy.wait()
    rows = starts_ref[...].astype(F32)
    marks = jnp.concatenate(
        [jnp.broadcast_to(rows[r : r + 1], (8, rows.shape[1])) for r in range(rows.shape[0])], axis=1
    )
    for q in range(n_block // 2):
        segs_ref[q] = spread_lanes(marks, q * PAIR)

    def both(ref, q, low):
        return jnp.concatenate([ref[2 * q, :, pl.ds(low, LANES)], ref[2 * q + 1, :, pl.ds(low, LANES)]], axis=0)

    @pl.loop(0, n_block // 2)
    def _(q):
        score, score_t = score_pair(segs_ref[q], both(b_ref, q, 0), both(c_ref, q, 0))
        score_ref[q] = score
        score_t_ref[q] = score_t
        one, two = pack_scores(score_t)
        tile_ref[2 * q] = one.astype(BF16)
        tile_ref[2 * q + 1] = two.astype(BF16)

    def label_of(s):
        target = grid.partner(s)
        label = jnp.int32(0)
        for block in range(n_block):
            label = label + jnp.where(plan_ref[block] == target, block + 1, 0)
        return label

    def outgoing(s):
        return remote(send_ref.at[s], got_ref.at[s], es_sem.at[s], er_sem.at[s], {"dp": grid.partner(s)})

    def noted(s):
        return remote(note_ref.at[s], notes_ref.at[s], ns_sem.at[s], nr_sem.at[s], {"dp": grid.partner(s)})

    @pl.loop(0, n_dp)
    def _(s):
        block = jnp.clip(label_of(s) - 1, 0, n_block - 1)
        whole = go_ref[block]
        for r in range(3):
            for t in range(4):
                send_ref[s, 4 * r + t] = whole[16 * r : 16 * r + 16, t * LANES : (t + 1) * LANES]
        send_ref[s, TILES - 1] = tile_ref[block]

    n_far = n_dp // 2

    def batch(index):
        for low, count, ends in ((0, n_far, FAR_ENDS), (n_far, n_dp - 1 - n_far, NEAR_ENDS)):
            begin = low + (ends[index - 1] * count // ends[-1] if index else 0)
            end = low + ends[index] * count // ends[-1]
            if end > begin:
                @pl.loop(begin, end)
                def _(s):
                    outgoing(s).start()

    own = pltpu.make_async_copy(send_ref.at[n_dp - 1], got_ref.at[n_dp - 1], own_sem.at[0])
    own.start()

    w_here = w_ref[...].astype(F32).T.astype(BF16)
    for copy in loads[3:]:
        copy.wait()
    weight_swap.wait()
    batch(0)
    w_other = wo_ref[...].astype(F32).T.astype(BF16)
    for copy in token_copies:
        copy.wait()
    full_ref[...] = lax.dot_general(w_here, xg_ref[0], NT, preferred_element_type=F32) + lax.dot_general(
        w_other, xg_ref[1], NT, preferred_element_type=F32
    )
    copies = []
    for step in list(range(1, n_z)) + [0]:
        for side in range(2):
            owner = (yh if side == 0 else 1 - yh) * n_z + (z + step) % n_z
            part_ref[step, side * 8 : (side + 1) * 8] = full_ref[pl.ds(pl.multiple_of(owner * 8, 8), 8)]
        if step:
            copy = remote(part_ref.at[step], rs_ref.at[step], ps_sem.at[step], pr_sem.at[step], at_z(step))
            copy.start()
            copies.append(copy)
    for side in range(2):
        xt_ref[side] = xg_ref[side].astype(F32).T.astype(BF16)
    total = part_ref[0]
    for step, copy in enumerate(copies, 1):
        copy.wait()
        total = total + rs_ref[step]
    give_ref[...] = total[8:]
    logit_swap = remote(give_ref, take_ref, ss_sem, sr_sem, across)
    logit_swap.start()
    for q in range(per_half):
        pre_ref[yh * per_half + q] = spread_lanes(total[:8], q * PAIR)

    rate = per_head(rate_ref, shard * 8)
    bias = per_head(bias_ref, shard * 8)
    lane = lanes()

    def work(*pairs):
        done = [
            mixer_pair(
                pre_ref[q], score_ref[q], score_t_ref[q], rate, bias,
                lambda duo, q=q: both(x_ref, q, duo * LANES), lambda duo, q=q: both(go_ref, q, duo * LANES),
            )
            for q in pairs
        ]
        for q, (grad_pre, level, step) in zip(pairs, done):
            gps_ref[q] = grad_pre
            level_ref[2 * q] = jnp.where(lane < BLK, level, pltpu.roll(step, BLK, 1))
            level_ref[2 * q + 1] = jnp.where(lane < BLK, pltpu.roll(level, LANES - BLK, 1), step)

    def work_span(low, count):
        if count % 2:
            @pl.loop(0, count)
            def _(q):
                work(low + q)
        elif count:
            @pl.loop(0, count // 2)
            def _(q):
                work(low + 2 * q, low + 2 * q + 1)

    work_span(yh * per_half, per_half // 2)
    logit_swap.wait()
    others = take_ref[...]
    for q in range(per_half):
        pre_ref[(1 - yh) * per_half + q] = spread_lanes(others, q * PAIR)

    batch(1)
    work_span((1 - yh) * per_half, per_half)

    half_ref[0] = gather_lanes([gps_ref[(1 - yh) * per_half + i] for i in range(per_half)])
    grad_swap = remote(half_ref.at[0], swap_ref, ws_sem, wr_sem, across)
    grad_swap.start()

    work_span(yh * per_half + per_half // 2, per_half - per_half // 2)

    mine_half = gather_lanes([gps_ref[yh * per_half + i] for i in range(per_half)])
    grad_swap.wait()
    msg_ref[...] = jnp.concatenate([mine_half, swap_ref[...]], axis=0).astype(BF16)
    copies = []
    for step in range(1, n_z):
        copy = remote(msg_ref, all_ref.at[step], gs_sem.at[step], gr_sem.at[step], at_z(step))
        copy.start()
        copies.append(copy)

    batch(2)

    @pl.loop(0, n_dp)
    def _(s):
        label = label_of(s)
        note_ref[s] = jnp.where(lane < PAIR, level_ref[jnp.clip(label - 1, 0, n_block - 1)], label.astype(F32))

        @pl.when(s < n_dp - 1)
        def _():
            noted(s).start()

    own_note = pltpu.make_async_copy(note_ref.at[n_dp - 1], notes_ref.at[n_dp - 1], own_sem.at[1])
    own_note.start()

    for step in range(n_z):
        if step:
            copies[step - 1].wait()
        message = (all_ref[step] if step else msg_ref[...]).astype(F32)
        place = (z + n_z - step) % n_z
        heads_ref[yh, place] = message[:8]
        heads_ref[1 - yh, place] = message[8:]
    grad_heads = heads_ref[...].reshape(2 * n_z * 8, heads_ref.shape[-1]).astype(BF16)
    unit = dw_ref.shape[0] // n_dp
    piece = n_y * unit
    for side in range(2):
        product = lax.dot_general(xt_ref[side], grad_heads, NT, preferred_element_type=F32)
        for c in range(2):
            for x in range(n_x):
                for y in range(n_y):
                    low = ((c * n_x + x) * n_y + y) * unit
                    d_ref[c, x, y, side] = product[low : low + unit]
    copy = remote(d_ref.at[1 - core], e1_ref, cs_sem, cr_sem, sibling)
    copy.start()
    copy.wait()
    a1_ref[...] = d_ref[core] + e1_ref[...]
    copies = []
    for step_x, step_y in plane[::-1]:
        for side in (1, 0):
            if side or step_x or step_y:
                copy = remote(
                    a1_ref.at[(xx + step_x) % n_x, (yy + step_y) % n_y, side], e2_ref.at[step_x, step_y, side],
                    xs_sem.at[step_x, step_y, side], xr_sem.at[step_x, step_y, side], at_xy(side, step_x, step_y),
                )
                copy.start()
                copies.append((step_x, step_y, side, copy))
    total = a1_ref[xx, yy, 0]
    for step_x, step_y, side, copy in copies:
        copy.wait()
        total = total + e2_ref[step_x, step_y, side]
    side_rows = n_x * piece
    low = pl.multiple_of(core * side_rows, side_rows)
    mine = pl.ds(pl.multiple_of(low + (xx * n_y + yy) * unit, unit), unit)
    dw_ref[mine] = total * (float(n_dp * n_block * BLK) ** -0.5)
    copies = []
    for step_x, step_y in plane[:0:-1]:
        copy = remote(
            dw_ref.at[mine], dw_ref.at[mine], hs_sem.at[step_x, step_y], hr_sem.at[step_x, step_y],
            at_xy(0, step_x, step_y),
        )
        copy.start()
        copies.append(copy)
    batch(3)
    for copy in copies:
        copy.wait()
    mine = pl.ds(low, side_rows)
    copy = remote(dw_ref.at[mine], dw_ref.at[mine], ks_sem, kr_sem, sibling)
    copy.start()
    copy.wait()

    @pl.loop(0, n_dp - 1)
    def _(s):
        noted(s).wait()
        outgoing(s).wait()

    own.wait()
    own_note.wait()


def main_call(grid, tokens, weight, x, go, b, c, starts, plan, bias, rate):
    n_block, _, width = x.shape
    n_z, n_x, n_y, n_dp = grid.n_z, grid.n_x, grid.n_y, grid.n_dp
    half = n_z * BLK
    feats, heads = weight.shape
    unit = feats // n_dp
    n_pair = n_block // 2
    dma = pltpu.SemaphoreType.DMA
    vmem = pl.BlockSpec(memory_space=pltpu.VMEM)
    smem = pl.BlockSpec(memory_space=pltpu.SMEM)
    hbm = pl.BlockSpec(memory_space=pl.ANY)
    return pl.pallas_call(
        functools.partial(main_kernel, grid, n_block),
        out_shape=(
            jax.ShapeDtypeStruct((n_dp, TILES, 16, LANES), BF16),
            jax.ShapeDtypeStruct((n_dp, 8, LANES), F32),
            jax.ShapeDtypeStruct((feats, heads), F32),
        ),
        in_specs=[hbm, vmem, hbm, hbm, hbm, hbm, vmem, smem, smem, smem],
        out_specs=[hbm, hbm, vmem],
        scratch_shapes=[
            pltpu.VMEM((2, half, feats), BF16),
            pltpu.VMEM((feats, heads), BF16),
            pltpu.VMEM((heads, half), F32),
            pltpu.VMEM((n_z, 16, half), F32),
            pltpu.VMEM((n_z, 16, half), F32),
            pltpu.VMEM((8, half), F32),
            pltpu.VMEM((8, half), F32),
            pltpu.VMEM((n_block, BLK, width), BF16),
            pltpu.VMEM((n_block, BLK, width), BF16),
            pltpu.VMEM((n_block, BLK, N), BF16),
            pltpu.VMEM((n_block, BLK, N), BF16),
            pltpu.VMEM((n_dp, TILES, 16, LANES), BF16),
            pltpu.VMEM((n_pair, 8, LANES), F32),
            pltpu.VMEM((n_pair, 8, LANES), F32),
            pltpu.VMEM((n_pair, PAIR, LANES), F32),
            pltpu.VMEM((n_pair, PAIR, LANES), F32),
            pltpu.VMEM((n_block, 16, LANES), BF16),
            pltpu.VMEM((n_block, 8, LANES), F32),
            pltpu.VMEM((n_dp, 8, LANES), F32),
            pltpu.VMEM((n_pair, 8, LANES), F32),
            pltpu.VMEM((1, 8, half), F32),
            pltpu.VMEM((8, half), F32),
            pltpu.VMEM((16, half), BF16),
            pltpu.VMEM((n_z, 16, half), BF16),
            pltpu.VMEM((2, n_z, 8, half), F32),
            pltpu.VMEM((2, feats, half), BF16),
            pltpu.VMEM((2, n_x, n_y, 2, unit, heads), F32),
            pltpu.VMEM((n_x, n_y, 2, unit, heads), F32),
            pltpu.VMEM((n_x, n_y, 2, unit, heads), F32),
            pltpu.VMEM((n_x, n_y, 2, unit, heads), F32),
            dma((2,)), dma((4,)), dma, dma, dma((n_z, 2)), dma((n_z, 2)), dma((n_z,)), dma((n_z,)), dma, dma,
            dma((n_dp,)), dma((n_dp,)), dma((n_dp,)), dma((n_dp,)), dma, dma, dma((n_z,)), dma((n_z,)), dma, dma,
            dma((n_x, n_y, 2)), dma((n_x, n_y, 2)), dma((n_x, n_y)), dma((n_x, n_y)), dma, dma, dma((2,)),
        ],
        compiler_params=pltpu.CompilerParams(
            collective_id=0, has_side_effects=True, vmem_limit_bytes=60 * 1024 * 1024
        ),
        cost_estimate=pl.CostEstimate(flops=10**9, bytes_accessed=10**7, transcendentals=10**6),
    )(tokens, weight, x, go, b, c, starts, plan, bias, rate)


def finish_kernel(gain_ref, got_ref, note_ref, dw_in_ref, out_ref, dw_ref, source_ref):
    shard = lax.axis_index("shard")
    lane = lanes()
    n_slot, n_block = got_ref.shape[0], out_ref.shape[0]
    labels = note_ref[:, 0, :]
    slot = lax.broadcasted_iota(jnp.int32, labels.shape, 0).astype(F32)
    labels = jnp.where(lax.broadcasted_iota(jnp.int32, labels.shape, 1) == LANES - 1, labels, 0.0)
    for block in range(n_block):
        found = jnp.sum(jnp.where(labels == float(block + 1), slot, 0.0))
        source_ref[block] = jnp.clip(found.astype(jnp.int32), 0, n_slot - 1)
    dw_ref[...] = dw_in_ref[...]
    away_t = causal(True)
    pad = jnp.zeros((LANES - PAIR, LANES), BF16)
    low_half = lax.broadcasted_iota(jnp.int32, (PAIR, LANES), 1) < 64

    def formed(q):
        first, second = source_ref[2 * q], source_ref[2 * q + 1]
        one, two = note_ref[first], note_ref[second]
        level = jnp.where(lane < BLK, one, jnp.where(lane < PAIR, pltpu.roll(two, BLK, 1), 0.0))
        step = jnp.where(lane < BLK, pltpu.roll(one, LANES - BLK, 1), jnp.where(lane < PAIR, two, 0.0))
        cols = columns_of(level, step)
        score_t = unpack_scores(
            got_ref[first, TILES - 1].astype(F32), got_ref[second, TILES - 1].astype(F32)
        )
        grads = []
        for duo in range(4):
            mix_t = []
            for head in (2 * duo, 2 * duo + 1):
                level_col = cols[:PAIR, head : head + 1]
                step_col = cols[:PAIR, 8 + head : 9 + head]
                mix_t.append(
                    (score_t * jnp.exp(level[head : head + 1] - level_col + away_t) * step_col).astype(BF16)
                )
            go = jnp.concatenate(
                [got_ref[first, 4 * r + duo] for r in range(3)] + [got_ref[second, 4 * r + duo] for r in range(3)],
                axis=0,
            )
            gv = lax.dot_general(
                jnp.concatenate(mix_t, axis=0), jnp.concatenate([go, pad], axis=0), NN, preferred_element_type=F32
            )
            gv = jnp.where(low_half, gv[:PAIR], gv[PAIR:])
            gain = jnp.where(low_half, gain_ref[shard * 8 + 2 * duo], gain_ref[shard * 8 + 2 * duo + 1])
            grads.append((gv + gain * go.astype(F32)).astype(BF16))
        return grads

    width = 2 if n_block % 4 == 0 else 1

    @pl.loop(0, n_block // 2 // width)
    def _(k):
        pairs = [width * k + i for i in range(width)]
        done = [formed(q) for q in pairs]
        for q, grads in zip(pairs, done):
            for duo, grad in enumerate(grads):
                out_ref[2 * q, :, duo * LANES : (duo + 1) * LANES] = grad[:BLK]
                out_ref[2 * q + 1, :, duo * LANES : (duo + 1) * LANES] = grad[BLK:]


def finish(gain, got, notes, dw, n_block):
    vmem = pl.BlockSpec(memory_space=pltpu.VMEM)
    smem = pl.BlockSpec(memory_space=pltpu.SMEM)
    return pl.pallas_call(
        finish_kernel,
        out_shape=(
            jax.ShapeDtypeStruct((n_block, BLK, 4 * LANES), BF16),
            jax.ShapeDtypeStruct(dw.shape, F32),
        ),
        in_specs=[smem, vmem, vmem, vmem],
        out_specs=[vmem, vmem],
        scratch_shapes=[pltpu.SMEM((n_block,), jnp.int32)],
        compiler_params=pltpu.CompilerParams(vmem_limit_bytes=60 * 1024 * 1024),
        cost_estimate=pl.CostEstimate(flops=10**8, bytes_accessed=4 * 10**6, transcendentals=10**6),
    )(gain, got, notes, dw)


def on_device(
    residual_in, conv_out, b_proj, c_proj, grad_out, doc_starts, dest_plan, dt_weight, dt_bias, decay_rate, skip_gain
):
    n_data = lax.axis_size("dp")
    grid = Grid(n_data, lax.axis_size("shard"))
    rows = conv_out.shape[0]
    n_block = rows // BLK

    def blocked(values):
        return values.reshape(n_block, BLK, -1)

    got, notes, dw = main_call(
        grid, residual_in, dt_weight, blocked(conv_out), blocked(grad_out), blocked(b_proj), blocked(c_proj),
        doc_starts.reshape(-1, math.gcd(rows, LANES)), dest_plan, dt_bias, decay_rate,
    )
    conv_grad, dw = finish(skip_gain, got, notes, dw, n_block)
    return conv_grad.reshape(rows, -1), dw


def solution(mesh):
    placed = (
        P(("dp", "shard"), None),
        P("dp", "shard"),
        P("dp", None),
        P("dp", None),
        P("dp", "shard"),
        P("dp"),
        P("dp"),
        P("shard", None),
        P(),
        P(),
        P(),
    )
    return jax.shard_map(
        on_device,
        mesh=mesh,
        in_specs=placed,
        out_specs=(P("dp", "shard"), P("shard", None)),
        check_vma=False,
    )
```

```python
import functools
import math

import jax
import jax.numpy as jnp
from jax import lax
from jax.experimental import pallas as pl
from jax.experimental.pallas import tpu as pltpu
from jax.sharding import PartitionSpec as P

N = 128
G = 4
BLK = 48
LANES = 128
MESH = pl.DeviceIdType.MESH
F32 = jnp.float32
BF16 = jnp.bfloat16
NT = (((1,), (1,)), ((), ()))
NN = (((1,), (0,)), ((), ()))
N_YHI = 2
PAIR = 2 * BLK
TILES = 13
FAR = -1e30
FAR_ENDS = (8, 9, 14, 16)
NEAR_ENDS = (6, 8, 14, 15)


class Grid:
    def __init__(self, n_dp, n_shard):
        self.n_dp = n_dp
        self.n_z = n_shard // N_YHI
        self.n_core = 2
        rest = n_dp // 2
        self.n_hb = 2 if rest >= 2 else 1
        rest //= self.n_hb
        self.n_x = min(rest, 4)
        self.n_lb = rest // self.n_x
        self.n_y = self.n_hb * self.n_lb

    def here(self):
        dp = lax.axis_index("dp")
        shard = lax.axis_index("shard")
        core = lax.rem(dp, self.n_core)
        x = lax.rem(dp // self.n_core, self.n_x)
        y = dp // (self.n_core * self.n_x)
        return dp, y, x, core, shard // self.n_z, lax.rem(shard, self.n_z)

    def dp_of(self, y, x, core):
        return (y * self.n_x + x) * self.n_core + core

    def partner(self, s):
        _, y, x, core, _, _ = self.here()
        mc = self.n_core - 1 - s % self.n_core
        mx = self.n_x - 1 - (s // self.n_core) % self.n_x
        t = s // (self.n_core * self.n_x)
        hb = y // self.n_lb
        lb = y % self.n_lb
        hb2 = (hb + self.n_hb - 1 + t // self.n_lb) % self.n_hb
        lb2 = (lb + self.n_lb - 1 + t % self.n_lb) % self.n_lb
        if self.n_lb == 1:
            lb2 = lb
        return self.dp_of(hb2 * self.n_lb + lb2, (x + mx) % self.n_x, (core + mc) % self.n_core)


def remote(src, dst, send, recv, device):
    return pltpu.make_async_remote_copy(
        src_ref=src, dst_ref=dst, send_sem=send, recv_sem=recv, device_id=device, device_id_type=MESH
    )


def lanes():
    return lax.broadcasted_iota(jnp.int32, (8, LANES), 1)


def spread_lanes(whole, low):
    width = whole.shape[1]
    if width % LANES:
        return jnp.pad(whole[:, low : low + PAIR], ((0, 0), (0, LANES - PAIR)))
    tile, off = low // LANES, low % LANES
    first = whole[:, tile * LANES : (tile + 1) * LANES]
    if off == 0:
        return first
    first = pltpu.roll(first, LANES - off, 1)
    if off + PAIR <= LANES:
        return first
    second = pltpu.roll(whole[:, (tile + 1) * LANES : (tile + 2) * LANES], LANES - off, 1)
    return jnp.where(lanes() < LANES - off, first, second)


def gather_lanes(pieces):
    width = len(pieces) * PAIR
    if width % LANES:
        return jnp.concatenate([p[:, :PAIR] for p in pieces], axis=1)
    lane = lanes()
    tiles = [jnp.zeros((8, LANES), F32) for _ in range(width // LANES)]
    for index, piece in enumerate(pieces):
        low = index * PAIR
        tile, off = low // LANES, low % LANES
        moved = pltpu.roll(piece, off, 1) if off else piece
        tiles[tile] = jnp.where((lane >= off) & (lane < off + PAIR), moved, tiles[tile])
        if off + PAIR > LANES:
            tiles[tile + 1] = jnp.where(lane < off + PAIR - LANES, moved, tiles[tile + 1])
    return jnp.concatenate(tiles, axis=1)


def triangle(kind):
    row = lax.broadcasted_iota(jnp.int32, (LANES, LANES), 0)
    col = lax.broadcasted_iota(jnp.int32, (LANES, LANES), 1)
    same = (row < BLK) == (col < BLK)
    if kind == "all":
        keep = row <= col
    elif kind == "ahead":
        keep = (row <= col) & same
    else:
        keep = (row >= col) & same
    return jnp.where(keep, 1.0, 0.0).astype(F32)


def causal(transposed):
    row = lax.broadcasted_iota(jnp.int32, (PAIR, LANES), 0)
    col = lax.broadcasted_iota(jnp.int32, (PAIR, LANES), 1)
    same = ((row < BLK) == (col < BLK)) & (col < PAIR)
    return jnp.where(same & ((row <= col) if transposed else (col <= row)), 0.0, FAR).astype(F32)


def exact_dot(a, b):
    return lax.dot_general(a, b, NN, preferred_element_type=F32, precision=lax.Precision.HIGHEST)


def columns_of(*rows):
    filled = LANES - 8 * len(rows)
    return jnp.concatenate(list(rows) + [jnp.zeros((filled, LANES), F32)], axis=0).T


def score_pair(starts, b, c):
    pad = jnp.zeros((LANES - PAIR, N), BF16)
    segment = lax.dot_general(
        starts.astype(BF16), triangle("all").astype(BF16), NN, preferred_element_type=F32
    )
    segment = jnp.where(lanes() < PAIR, segment, -1.0)
    same = columns_of(segment)[:PAIR, 0:1] == segment[0:1]
    score = lax.dot_general(c, jnp.concatenate([b, pad], axis=0), NT, preferred_element_type=F32)
    score_t = lax.dot_general(b, jnp.concatenate([c, pad], axis=0), NT, preferred_element_type=F32)
    return (
        jnp.where(same & (causal(False) == 0.0), score, 0.0),
        jnp.where(same & (causal(True) == 0.0), score_t, 0.0),
    )


def pack_scores(score_t):
    lane = lax.broadcasted_iota(jnp.int32, (16, LANES), 1)

    def packed(first, second, third):
        return jnp.where(lane < 48, first, jnp.where(lane < 96, second, third))

    return (
        packed(score_t[0:16], pltpu.roll(score_t[16:32], 48, 1), pltpu.roll(score_t[32:48], 64, 1)),
        packed(pltpu.roll(score_t[48:64], 80, 1), score_t[64:80], pltpu.roll(score_t[80:96], 16, 1)),
    )


def unpack_scores(one, two):
    return jnp.concatenate(
        [one, pltpu.roll(one, 80, 1), pltpu.roll(one, 64, 1), pltpu.roll(two, 48, 1), two, pltpu.roll(two, 112, 1)],
        axis=0,
    )


def product_pair(score, score_t, x_of, go_of):
    pad = jnp.zeros((LANES - PAIR, LANES), BF16)
    low_half = lax.broadcasted_iota(jnp.int32, (PAIR, LANES), 1) < 64

    def halves(rows):
        zero = jnp.zeros_like(rows)
        return jnp.concatenate([jnp.where(low_half, rows, zero), jnp.where(low_half, zero, rows)], axis=0)

    by_i, by_j = [], []
    for duo in range(4):
        x, go = x_of(duo), go_of(duo)
        wide = lax.dot_general(halves(go), jnp.concatenate([x, pad], axis=0), NT, preferred_element_type=F32)
        wide_t = lax.dot_general(halves(x), jnp.concatenate([go, pad], axis=0), NT, preferred_element_type=F32)
        for part in range(2):
            by_i.append(wide[part * PAIR : (part + 1) * PAIR] * score)
            by_j.append(wide_t[part * PAIR : (part + 1) * PAIR] * score_t)
    return by_i, by_j


def mixer_pair(pre, by_i, by_j, rate, bias):
    lane = lanes()
    row = lax.broadcasted_iota(jnp.int32, (8, LANES), 0)
    gate = jnp.where(lane < PAIR, pre + bias, 0.0)
    e = jnp.exp(-jnp.abs(gate))
    series = e * (1.0 - e * (0.5 - e * (1.0 / 3.0 - e * (0.25 - e * 0.2))))
    log1p = jnp.where(e < 0.02, series, jnp.log(1.0 + e))
    step = jnp.maximum(gate, 0.0) + log1p
    sig = jnp.where(gate >= 0, 1.0, e) / (1.0 + e)
    level = exact_dot(jnp.where(lane < PAIR, -step * rate, 0.0), triangle("ahead"))
    cols = columns_of(level, step)
    away, away_t = causal(False), causal(True)
    grad_step = jnp.zeros((8, LANES), F32)
    outflow = jnp.zeros((8, LANES), F32)
    for head in range(8):
        level_col = cols[:PAIR, head : head + 1]
        step_col = cols[:PAIR, 8 + head : 9 + head]
        level_row = level[head : head + 1]
        weighted = by_i(head) * jnp.exp(level_col - level_row + away)
        flow = by_j(head) * jnp.exp(level_row - level_col + away_t) * step_col
        grad_step = jnp.where(row == head, jnp.sum(weighted, axis=0, keepdims=True), grad_step)
        outflow = jnp.where(row == head, jnp.sum(flow, axis=0, keepdims=True), outflow)
    grad_log = exact_dot(outflow - grad_step * step, triangle("behind"))
    return (grad_step - rate * grad_log) * sig, level, step


def per_head(ref, first_head):
    row = lax.broadcasted_iota(jnp.int32, (8, LANES), 0)
    out = jnp.zeros((8, LANES), F32)
    for head in range(8):
        out = jnp.where(row == head, ref[first_head + head], out)
    return out


def main_kernel(
    grid, n_block,
    tokens_any, w_ref, x_any, go_any, b_any, c_any, starts_ref, plan_ref, bias_ref, rate_ref,
    got_ref, notes_ref, dw_ref,
    stage_ref, xg_ref, wo_ref, full_ref, part_ref, rs_ref, give_ref, take_ref,
    x_ref, go_ref, b_ref, c_ref, send_ref, pre_ref, segs_ref, score_ref, score_t_ref, tile_ref, level_ref, note_ref,
    by_i_ref, by_j_ref, label_ref, gps_ref, half_ref, swap_ref, msg_ref, all_ref, heads_ref, xt_ref, d_ref, e1_ref, a1_ref, e2_ref,
    local_sem, load_sem, vs_sem, vr_sem, ts_sem, tr_sem, ps_sem, pr_sem, ss_sem, sr_sem,
    es_sem, er_sem, qs_sem, qr_sem, ns_sem, nr_sem, ws_sem, wr_sem, gs_sem, gr_sem, cs_sem, cr_sem, xs_sem, xr_sem,
    hs_sem, hr_sem, ks_sem, kr_sem, own_sem,
):
    n_z, n_x, n_y, n_dp = grid.n_z, grid.n_x, grid.n_y, grid.n_dp
    dp, yy, xx, core, yh, z = grid.here()
    shard = yh * n_z + z
    other = (1 - yh) * n_z + z
    across = {"shard": other}
    sibling = {"dp": grid.dp_of(yy, xx, 1 - core)}
    feats = w_ref.shape[0]
    per_half = n_z // 2

    def at_z(step):
        return {"shard": yh * n_z + (z + step) % n_z}

    def at_xy(side, step_x, step_y):
        place = grid.dp_of((yy + step_y) % n_y, (xx + step_x) % n_x, core)
        return {"dp": place, "shard": shard if side == 0 else other}

    plane = [(step_x, step_y) for step_x in range(n_x) for step_y in range(n_y)]

    barrier = pltpu.get_barrier_semaphore()
    for step in range(1, n_z):
        pl.semaphore_signal(barrier, inc=1, device_id=at_z(step), device_id_type=MESH)
    for step_x, step_y in plane:
        pl.semaphore_signal(barrier, inc=1, device_id=at_xy(1, step_x, step_y), device_id_type=MESH)

    @pl.loop(0, n_dp - 1)
    def _(s):
        pl.semaphore_signal(barrier, inc=1, device_id={"dp": grid.partner(s)}, device_id_type=MESH)

    def feature_columns(side, step):
        owner = (yh if side == 0 else 1 - yh) * n_z + (z + step) % n_z
        return tokens_any.at[:, pl.ds(pl.multiple_of(owner * feats, feats), feats)]

    group = (shard * 8) // (2 * n_z * 8 // G)
    cols = pl.ds(pl.multiple_of(group * N, N), N)
    staged = []
    for step in range(n_z):
        for side in range(2):
            target = stage_ref.at[step, side] if step else xg_ref.at[z, side]
            staged.append(pltpu.make_async_copy(feature_columns(side, step), target, local_sem.at[step, side]))
    for copy in staged:
        copy.start()
    loads = [
        pltpu.make_async_copy(b_any.at[:, :, cols], b_ref, load_sem.at[2]),
        pltpu.make_async_copy(c_any.at[:, :, cols], c_ref, load_sem.at[3]),
        pltpu.make_async_copy(go_any, go_ref, load_sem.at[1]),
        pltpu.make_async_copy(x_any, x_ref, load_sem.at[0]),
    ]
    for copy in loads:
        copy.start()
    pl.semaphore_wait(barrier, n_dp - 1 + n_z - 1 + n_x * n_y)

    mirrored = {"dp": grid.dp_of(n_y - 1 - yy, xx, core), "shard": other}
    weight_swap = remote(w_ref, wo_ref, vs_sem, vr_sem, mirrored)
    weight_swap.start()
    for copy in staged:
        copy.wait()
    token_copies = []
    for step in range(1, n_z):
        copy = remote(stage_ref.at[step], xg_ref.at[z], ts_sem.at[step], tr_sem.at[step], at_z(step))
        copy.start()
        token_copies.append(copy)

    def label_of(s):
        target = grid.partner(s)
        label = jnp.int32(0)
        for block in range(n_block):
            label = label + jnp.where(plan_ref[block] == target, block + 1, 0)
        return label

    def outgoing(s):
        body = pl.ds(0, TILES - 1)
        return remote(
            send_ref.at[s, body], got_ref.at[s, body], es_sem.at[s], er_sem.at[s], {"dp": grid.partner(s)}
        )

    def scored(s):
        return remote(
            send_ref.at[s, TILES - 1], got_ref.at[s, TILES - 1], qs_sem.at[s], qr_sem.at[s], {"dp": grid.partner(s)}
        )

    def noted(s):
        return remote(note_ref.at[s], notes_ref.at[s], ns_sem.at[s], nr_sem.at[s], {"dp": grid.partner(s)})

    def place(s):
        label = label_of(s)
        label_ref[s] = label
        whole = go_ref[jnp.clip(label - 1, 0, n_block - 1)]
        for r in range(3):
            for t in range(4):
                send_ref[s, 4 * r + t] = whole[16 * r : 16 * r + 16, t * LANES : (t + 1) * LANES]

    n_far = n_dp // 2

    def spans(index):
        for low, count, ends in ((0, n_far, FAR_ENDS), (n_far, n_dp - 1 - n_far, NEAR_ENDS)):
            begin = low + (ends[index - 1] * count // ends[-1] if index else 0)
            end = low + ends[index] * count // ends[-1]
            if end > begin:
                yield begin, end

    def batch(index):
        for begin, end in spans(index):
            @pl.loop(begin, end)
            def _(s):
                outgoing(s).start()

    loads[2].wait()
    for begin, end in spans(0):
        @pl.loop(begin, end)
        def _(s):
            place(s)
            outgoing(s).start()

    for index in (1, 2, 3):
        for begin, end in spans(index):
            @pl.loop(begin, end)
            def _(s):
                place(s)

    place(n_dp - 1)

    for copy in loads[:2]:
        copy.wait()
    rows = starts_ref[...].astype(F32)
    marks = jnp.concatenate(
        [jnp.broadcast_to(rows[r : r + 1], (8, rows.shape[1])) for r in range(rows.shape[0])], axis=1
    )
    for q in range(n_block // 2):
        segs_ref[q] = spread_lanes(marks, q * PAIR)

    def both(ref, q, low):
        return jnp.concatenate([ref[2 * q, :, pl.ds(low, LANES)], ref[2 * q + 1, :, pl.ds(low, LANES)]], axis=0)

    @pl.loop(0, n_block // 2)
    def _(q):
        score, score_t = score_pair(segs_ref[q], both(b_ref, q, 0), both(c_ref, q, 0))
        score_ref[q] = score
        score_t_ref[q] = score_t
        one, two = pack_scores(score_t)
        tile_ref[2 * q] = one.astype(BF16)
        tile_ref[2 * q + 1] = two.astype(BF16)

    @pl.loop(0, n_dp)
    def _(s):
        send_ref[s, TILES - 1] = tile_ref[jnp.clip(label_ref[s] - 1, 0, n_block - 1)]

    own = pltpu.make_async_copy(send_ref.at[n_dp - 1], got_ref.at[n_dp - 1], own_sem.at[0])
    own.start()

    w_here = w_ref[...].astype(F32).T.astype(BF16)
    for copy in loads[3:]:
        copy.wait()

    @pl.loop(0, n_block // 2)
    def _(q):
        by_i, by_j = product_pair(
            score_ref[q], score_t_ref[q],
            lambda duo: both(x_ref, q, duo * LANES), lambda duo: both(go_ref, q, duo * LANES),
        )
        for head in range(8):
            by_i_ref[q, head] = by_i[head]
            by_j_ref[q, head] = by_j[head]

    weight_swap.wait()
    w_other = wo_ref[...].astype(F32).T.astype(BF16)
    for copy in token_copies:
        copy.wait()
    columns = [xg_ref[:, side].reshape(n_z * BLK, feats) for side in range(2)]
    full_ref[...] = lax.dot_general(w_here, columns[0], NT, preferred_element_type=F32) + lax.dot_general(
        w_other, columns[1], NT, preferred_element_type=F32
    )
    copies = []
    for step in list(range(1, n_z)) + [0]:
        for side in range(2):
            owner = (yh if side == 0 else 1 - yh) * n_z + (z + step) % n_z
            part_ref[step, side * 8 : (side + 1) * 8] = full_ref[pl.ds(pl.multiple_of(owner * 8, 8), 8)]
        if step:
            copy = remote(part_ref.at[step], rs_ref.at[step], ps_sem.at[step], pr_sem.at[step], at_z(step))
            copy.start()
            copies.append(copy)
    for side in range(2):
        xt_ref[side] = columns[side].astype(F32).T.astype(BF16)
    total = part_ref[0]
    for step, copy in enumerate(copies, 1):
        copy.wait()
        total = total + rs_ref[step]
    give_ref[...] = total[8:]
    logit_swap = remote(give_ref, take_ref, ss_sem, sr_sem, across)
    logit_swap.start()
    for q in range(per_half):
        pre_ref[yh * per_half + q] = spread_lanes(total[:8], q * PAIR)

    rate = per_head(rate_ref, shard * 8)
    bias = per_head(bias_ref, shard * 8)
    lane = lanes()

    def work(*pairs):
        done = [
            mixer_pair(
                pre_ref[q], lambda head, q=q: by_i_ref[q, head], lambda head, q=q: by_j_ref[q, head], rate, bias
            )
            for q in pairs
        ]
        for q, (grad_pre, level, step) in zip(pairs, done):
            gps_ref[q] = grad_pre
            level_ref[2 * q] = jnp.where(lane < BLK, level, pltpu.roll(step, BLK, 1))
            level_ref[2 * q + 1] = jnp.where(lane < BLK, pltpu.roll(level, LANES - BLK, 1), step)

    def work_span(low, count):
        if count % 2:
            @pl.loop(0, count)
            def _(q):
                work(low + q)
        elif count:
            @pl.loop(0, count // 2)
            def _(q):
                work(low + 2 * q, low + 2 * q + 1)

    work_span(yh * per_half, per_half // 2)
    logit_swap.wait()
    others = take_ref[...]
    for q in range(per_half):
        pre_ref[(1 - yh) * per_half + q] = spread_lanes(others, q * PAIR)

    batch(1)
    work_span((1 - yh) * per_half, per_half)

    half_ref[0] = gather_lanes([gps_ref[(1 - yh) * per_half + i] for i in range(per_half)])
    grad_swap = remote(half_ref.at[0], swap_ref, ws_sem, wr_sem, across)
    grad_swap.start()

    work_span(yh * per_half + per_half // 2, per_half - per_half // 2)

    mine_half = gather_lanes([gps_ref[yh * per_half + i] for i in range(per_half)])
    grad_swap.wait()
    msg_ref[...] = jnp.concatenate([mine_half, swap_ref[...]], axis=0).astype(BF16)
    copies = []
    for step in range(1, n_z):
        copy = remote(msg_ref, all_ref.at[step], gs_sem.at[step], gr_sem.at[step], at_z(step))
        copy.start()
        copies.append(copy)

    batch(2)

    @pl.loop(0, n_dp)
    def _(s):
        label = label_ref[s]
        note_ref[s] = jnp.where(lane < PAIR, level_ref[jnp.clip(label - 1, 0, n_block - 1)], label.astype(F32))

        @pl.when(s < n_dp - 1)
        def _():
            scored(s).start()
            noted(s).start()

    own_note = pltpu.make_async_copy(note_ref.at[n_dp - 1], notes_ref.at[n_dp - 1], own_sem.at[1])
    own_note.start()

    for step in range(n_z):
        if step:
            copies[step - 1].wait()
        message = (all_ref[step] if step else msg_ref[...]).astype(F32)
        place = (z + n_z - step) % n_z
        heads_ref[yh, place] = message[:8]
        heads_ref[1 - yh, place] = message[8:]
    grad_heads = heads_ref[...].reshape(2 * n_z * 8, heads_ref.shape[-1]).astype(BF16)
    unit = dw_ref.shape[0] // n_dp
    piece = n_y * unit
    for side in range(2):
        product = lax.dot_general(xt_ref[side], grad_heads, NT, preferred_element_type=F32)
        for c in range(2):
            for x in range(n_x):
                for y in range(n_y):
                    low = ((c * n_x + x) * n_y + y) * unit
                    d_ref[c, x, y, side] = product[low : low + unit]
    copy = remote(d_ref.at[1 - core], e1_ref, cs_sem, cr_sem, sibling)
    copy.start()
    copy.wait()
    a1_ref[...] = d_ref[core] + e1_ref[...]
    copies = []
    for step_x, step_y in plane[::-1]:
        for side in (1, 0):
            if side or step_x or step_y:
                copy = remote(
                    a1_ref.at[(xx + step_x) % n_x, (yy + step_y) % n_y, side], e2_ref.at[step_x, step_y, side],
                    xs_sem.at[step_x, step_y, side], xr_sem.at[step_x, step_y, side], at_xy(side, step_x, step_y),
                )
                copy.start()
                copies.append((step_x, step_y, side, copy))
    total = a1_ref[xx, yy, 0]
    for step_x, step_y, side, copy in copies:
        copy.wait()
        total = total + e2_ref[step_x, step_y, side]
    side_rows = n_x * piece
    low = pl.multiple_of(core * side_rows, side_rows)
    mine = pl.ds(pl.multiple_of(low + (xx * n_y + yy) * unit, unit), unit)
    dw_ref[mine] = total * (float(n_dp * n_block * BLK) ** -0.5)
    copies = []
    for step_x, step_y in plane[:0:-1]:
        copy = remote(
            dw_ref.at[mine], dw_ref.at[mine], hs_sem.at[step_x, step_y], hr_sem.at[step_x, step_y],
            at_xy(0, step_x, step_y),
        )
        copy.start()
        copies.append(copy)
    batch(3)
    for copy in copies:
        copy.wait()
    mine = pl.ds(low, side_rows)
    copy = remote(dw_ref.at[mine], dw_ref.at[mine], ks_sem, kr_sem, sibling)
    copy.start()
    copy.wait()

    @pl.loop(0, n_dp - 1)
    def _(s):
        scored(s).wait()
        noted(s).wait()
        outgoing(s).wait()

    own.wait()
    own_note.wait()


def main_call(grid, tokens, weight, x, go, b, c, starts, plan, bias, rate):
    n_block, _, width = x.shape
    n_z, n_x, n_y, n_dp = grid.n_z, grid.n_x, grid.n_y, grid.n_dp
    half = n_z * BLK
    feats, heads = weight.shape
    unit = feats // n_dp
    n_pair = n_block // 2
    dma = pltpu.SemaphoreType.DMA
    vmem = pl.BlockSpec(memory_space=pltpu.VMEM)
    smem = pl.BlockSpec(memory_space=pltpu.SMEM)
    hbm = pl.BlockSpec(memory_space=pl.ANY)
    return pl.pallas_call(
        functools.partial(main_kernel, grid, n_block),
        out_shape=(
            jax.ShapeDtypeStruct((n_dp, TILES, 16, LANES), BF16),
            jax.ShapeDtypeStruct((n_dp, 8, LANES), F32),
            jax.ShapeDtypeStruct((feats, heads), F32),
        ),
        in_specs=[hbm, vmem, hbm, hbm, hbm, hbm, vmem, smem, smem, smem],
        out_specs=[hbm, hbm, vmem],
        scratch_shapes=[
            pltpu.VMEM((n_z, 2, BLK, feats), BF16),
            pltpu.VMEM((n_z, 2, BLK, feats), BF16),
            pltpu.VMEM((feats, heads), BF16),
            pltpu.VMEM((heads, half), F32),
            pltpu.VMEM((n_z, 16, half), F32),
            pltpu.VMEM((n_z, 16, half), F32),
            pltpu.VMEM((8, half), F32),
            pltpu.VMEM((8, half), F32),
            pltpu.VMEM((n_block, BLK, width), BF16),
            pltpu.VMEM((n_block, BLK, width), BF16),
            pltpu.VMEM((n_block, BLK, N), BF16),
            pltpu.VMEM((n_block, BLK, N), BF16),
            pltpu.VMEM((n_dp, TILES, 16, LANES), BF16),
            pltpu.VMEM((n_pair, 8, LANES), F32),
            pltpu.VMEM((n_pair, 8, LANES), F32),
            pltpu.VMEM((n_pair, PAIR, LANES), F32),
            pltpu.VMEM((n_pair, PAIR, LANES), F32),
            pltpu.VMEM((n_block, 16, LANES), BF16),
            pltpu.VMEM((n_block, 8, LANES), F32),
            pltpu.VMEM((n_dp, 8, LANES), F32),
            pltpu.VMEM((n_pair, 8, PAIR, LANES), F32),
            pltpu.VMEM((n_pair, 8, PAIR, LANES), F32),
            pltpu.SMEM((n_dp,), jnp.int32),
            pltpu.VMEM((n_pair, 8, LANES), F32),
            pltpu.VMEM((1, 8, half), F32),
            pltpu.VMEM((8, half), F32),
            pltpu.VMEM((16, half), BF16),
            pltpu.VMEM((n_z, 16, half), BF16),
            pltpu.VMEM((2, n_z, 8, half), F32),
            pltpu.VMEM((2, feats, half), BF16),
            pltpu.VMEM((2, n_x, n_y, 2, unit, heads), F32),
            pltpu.VMEM((n_x, n_y, 2, unit, heads), F32),
            pltpu.VMEM((n_x, n_y, 2, unit, heads), F32),
            pltpu.VMEM((n_x, n_y, 2, unit, heads), F32),
            dma((n_z, 2)), dma((4,)), dma, dma, dma((n_z,)), dma((n_z,)), dma((n_z,)), dma((n_z,)), dma, dma,
            dma((n_dp,)), dma((n_dp,)), dma((n_dp,)), dma((n_dp,)), dma((n_dp,)), dma((n_dp,)), dma, dma, dma((n_z,)), dma((n_z,)), dma, dma,
            dma((n_x, n_y, 2)), dma((n_x, n_y, 2)), dma((n_x, n_y)), dma((n_x, n_y)), dma, dma, dma((2,)),
        ],
        compiler_params=pltpu.CompilerParams(
            collective_id=0, has_side_effects=True, vmem_limit_bytes=60 * 1024 * 1024
        ),
        cost_estimate=pl.CostEstimate(flops=10**9, bytes_accessed=10**7, transcendentals=10**6),
    )(tokens, weight, x, go, b, c, starts, plan, bias, rate)


def finish_kernel(gain_ref, got_ref, note_ref, dw_in_ref, out_ref, dw_ref, source_ref):
    shard = lax.axis_index("shard")
    lane = lanes()
    n_slot, n_block = got_ref.shape[0], out_ref.shape[0]
    labels = note_ref[:, 0, :]
    slot = lax.broadcasted_iota(jnp.int32, labels.shape, 0).astype(F32)
    labels = jnp.where(lax.broadcasted_iota(jnp.int32, labels.shape, 1) == LANES - 1, labels, 0.0)
    for block in range(n_block):
        found = jnp.sum(jnp.where(labels == float(block + 1), slot, 0.0))
        source_ref[block] = jnp.clip(found.astype(jnp.int32), 0, n_slot - 1)
    dw_ref[...] = dw_in_ref[...]
    away_t = causal(True)
    pad = jnp.zeros((LANES - PAIR, LANES), BF16)
    low_half = lax.broadcasted_iota(jnp.int32, (PAIR, LANES), 1) < 64

    def formed(q):
        first, second = source_ref[2 * q], source_ref[2 * q + 1]
        one, two = note_ref[first], note_ref[second]
        level = jnp.where(lane < BLK, one, jnp.where(lane < PAIR, pltpu.roll(two, BLK, 1), 0.0))
        step = jnp.where(lane < BLK, pltpu.roll(one, LANES - BLK, 1), jnp.where(lane < PAIR, two, 0.0))
        cols = columns_of(level, step)
        score_t = unpack_scores(
            got_ref[first, TILES - 1].astype(F32), got_ref[second, TILES - 1].astype(F32)
        )
        grads = []
        for duo in range(4):
            mix_t = []
            for head in (2 * duo, 2 * duo + 1):
                level_col = cols[:PAIR, head : head + 1]
                step_col = cols[:PAIR, 8 + head : 9 + head]
                mix_t.append(
                    (score_t * jnp.exp(level[head : head + 1] - level_col + away_t) * step_col).astype(BF16)
                )
            go = jnp.concatenate(
                [got_ref[first, 4 * r + duo] for r in range(3)] + [got_ref[second, 4 * r + duo] for r in range(3)],
                axis=0,
            )
            gv = lax.dot_general(
                jnp.concatenate(mix_t, axis=0), jnp.concatenate([go, pad], axis=0), NN, preferred_element_type=F32
            )
            gv = jnp.where(low_half, gv[:PAIR], gv[PAIR:])
            gain = jnp.where(low_half, gain_ref[shard * 8 + 2 * duo], gain_ref[shard * 8 + 2 * duo + 1])
            grads.append((gv + gain * go.astype(F32)).astype(BF16))
        return grads

    width = 2 if n_block % 4 == 0 else 1

    @pl.loop(0, n_block // 2 // width)
    def _(k):
        pairs = [width * k + i for i in range(width)]
        done = [formed(q) for q in pairs]
        for q, grads in zip(pairs, done):
            for duo, grad in enumerate(grads):
                out_ref[2 * q, :, duo * LANES : (duo + 1) * LANES] = grad[:BLK]
                out_ref[2 * q + 1, :, duo * LANES : (duo + 1) * LANES] = grad[BLK:]


def finish(gain, got, notes, dw, n_block):
    vmem = pl.BlockSpec(memory_space=pltpu.VMEM)
    smem = pl.BlockSpec(memory_space=pltpu.SMEM)
    return pl.pallas_call(
        finish_kernel,
        out_shape=(
            jax.ShapeDtypeStruct((n_block, BLK, 4 * LANES), BF16),
            jax.ShapeDtypeStruct(dw.shape, F32),
        ),
        in_specs=[smem, vmem, vmem, vmem],
        out_specs=[vmem, vmem],
        scratch_shapes=[pltpu.SMEM((n_block,), jnp.int32)],
        compiler_params=pltpu.CompilerParams(vmem_limit_bytes=60 * 1024 * 1024),
        cost_estimate=pl.CostEstimate(flops=10**8, bytes_accessed=4 * 10**6, transcendentals=10**6),
    )(gain, got, notes, dw)


def on_device(
    residual_in, conv_out, b_proj, c_proj, grad_out, doc_starts, dest_plan, dt_weight, dt_bias, decay_rate, skip_gain
):
    n_data = lax.axis_size("dp")
    grid = Grid(n_data, lax.axis_size("shard"))
    rows = conv_out.shape[0]
    n_block = rows // BLK

    def blocked(values):
        return values.reshape(n_block, BLK, -1)

    got, notes, dw = main_call(
        grid, residual_in, dt_weight, blocked(conv_out), blocked(grad_out), blocked(b_proj), blocked(c_proj),
        doc_starts.reshape(-1, math.gcd(rows, LANES)), dest_plan, dt_bias, decay_rate,
    )
    conv_grad, dw = finish(skip_gain, got, notes, dw, n_block)
    return conv_grad.reshape(rows, -1), dw


def solution(mesh):
    placed = (
        P(("dp", "shard"), None),
        P("dp", "shard"),
        P("dp", None),
        P("dp", None),
        P("dp", "shard"),
        P("dp"),
        P("dp"),
        P("shard", None),
        P(),
        P(),
        P(),
    )
    return jax.shard_map(
        on_device,
        mesh=mesh,
        in_specs=placed,
        out_specs=(P("dp", "shard"), P("shard", None)),
        check_vma=False,
    )
```

```python
import functools
import math

import jax
import jax.numpy as jnp
from jax import lax
from jax.experimental import pallas as pl
from jax.experimental.pallas import tpu as pltpu
from jax.sharding import PartitionSpec as P

N = 128
G = 4
BLK = 48
LANES = 128
MESH = pl.DeviceIdType.MESH
F32 = jnp.float32
BF16 = jnp.bfloat16
NT = (((1,), (1,)), ((), ()))
NN = (((1,), (0,)), ((), ()))
N_YHI = 2
PAIR = 2 * BLK
TILES = 13
FAR = -1e30
FAR_ENDS = (8, 9, 14, 16)
NEAR_ENDS = (6, 8, 14, 15)


class Grid:
    def __init__(self, n_dp, n_shard):
        self.n_dp = n_dp
        self.n_z = n_shard // N_YHI
        self.n_core = 2
        rest = n_dp // 2
        self.n_hb = 2 if rest >= 2 else 1
        rest //= self.n_hb
        self.n_x = min(rest, 4)
        self.n_lb = rest // self.n_x
        self.n_y = self.n_hb * self.n_lb

    def here(self):
        dp = lax.axis_index("dp")
        shard = lax.axis_index("shard")
        core = lax.rem(dp, self.n_core)
        x = lax.rem(dp // self.n_core, self.n_x)
        y = dp // (self.n_core * self.n_x)
        return dp, y, x, core, shard // self.n_z, lax.rem(shard, self.n_z)

    def dp_of(self, y, x, core):
        return (y * self.n_x + x) * self.n_core + core

    def partner(self, s):
        _, y, x, core, _, _ = self.here()
        mc = self.n_core - 1 - s % self.n_core
        mx = self.n_x - 1 - (s // self.n_core) % self.n_x
        t = s // (self.n_core * self.n_x)
        hb = y // self.n_lb
        lb = y % self.n_lb
        hb2 = (hb + self.n_hb - 1 + t // self.n_lb) % self.n_hb
        lb2 = (lb + self.n_lb - 1 + t % self.n_lb) % self.n_lb
        if self.n_lb == 1:
            lb2 = lb
        return self.dp_of(hb2 * self.n_lb + lb2, (x + mx) % self.n_x, (core + mc) % self.n_core)


def remote(src, dst, send, recv, device):
    return pltpu.make_async_remote_copy(
        src_ref=src, dst_ref=dst, send_sem=send, recv_sem=recv, device_id=device, device_id_type=MESH
    )


def lanes():
    return lax.broadcasted_iota(jnp.int32, (8, LANES), 1)


def spread_lanes(whole, low):
    width = whole.shape[1]
    if width % LANES:
        return jnp.pad(whole[:, low : low + PAIR], ((0, 0), (0, LANES - PAIR)))
    tile, off = low // LANES, low % LANES
    first = whole[:, tile * LANES : (tile + 1) * LANES]
    if off == 0:
        return first
    first = pltpu.roll(first, LANES - off, 1)
    if off + PAIR <= LANES:
        return first
    second = pltpu.roll(whole[:, (tile + 1) * LANES : (tile + 2) * LANES], LANES - off, 1)
    return jnp.where(lanes() < LANES - off, first, second)


def gather_lanes(pieces):
    width = len(pieces) * PAIR
    if width % LANES:
        return jnp.concatenate([p[:, :PAIR] for p in pieces], axis=1)
    lane = lanes()
    tiles = [jnp.zeros((8, LANES), F32) for _ in range(width // LANES)]
    for index, piece in enumerate(pieces):
        low = index * PAIR
        tile, off = low // LANES, low % LANES
        moved = pltpu.roll(piece, off, 1) if off else piece
        tiles[tile] = jnp.where((lane >= off) & (lane < off + PAIR), moved, tiles[tile])
        if off + PAIR > LANES:
            tiles[tile + 1] = jnp.where(lane < off + PAIR - LANES, moved, tiles[tile + 1])
    return jnp.concatenate(tiles, axis=1)


def triangle(kind):
    row = lax.broadcasted_iota(jnp.int32, (LANES, LANES), 0)
    col = lax.broadcasted_iota(jnp.int32, (LANES, LANES), 1)
    same = (row < BLK) == (col < BLK)
    if kind == "all":
        keep = row <= col
    elif kind == "ahead":
        keep = (row <= col) & same
    else:
        keep = (row >= col) & same
    return jnp.where(keep, 1.0, 0.0).astype(F32)


def causal(transposed):
    row = lax.broadcasted_iota(jnp.int32, (PAIR, LANES), 0)
    col = lax.broadcasted_iota(jnp.int32, (PAIR, LANES), 1)
    same = ((row < BLK) == (col < BLK)) & (col < PAIR)
    return jnp.where(same & ((row <= col) if transposed else (col <= row)), 0.0, FAR).astype(F32)


def exact_dot(a, b):
    return lax.dot_general(a, b, NN, preferred_element_type=F32, precision=lax.Precision.HIGHEST)


def columns_of(*rows):
    filled = LANES - 8 * len(rows)
    return jnp.concatenate(list(rows) + [jnp.zeros((filled, LANES), F32)], axis=0).T


def score_pair(starts, b, c):
    pad = jnp.zeros((LANES - PAIR, N), BF16)
    segment = lax.dot_general(
        starts.astype(BF16), triangle("all").astype(BF16), NN, preferred_element_type=F32
    )
    segment = jnp.where(lanes() < PAIR, segment, -1.0)
    same = columns_of(segment)[:PAIR, 0:1] == segment[0:1]
    score = lax.dot_general(c, jnp.concatenate([b, pad], axis=0), NT, preferred_element_type=F32)
    score_t = lax.dot_general(b, jnp.concatenate([c, pad], axis=0), NT, preferred_element_type=F32)
    return (
        jnp.where(same & (causal(False) == 0.0), score, 0.0),
        jnp.where(same & (causal(True) == 0.0), score_t, 0.0),
    )


def pack_scores(score_t):
    lane = lax.broadcasted_iota(jnp.int32, (16, LANES), 1)

    def packed(first, second, third):
        return jnp.where(lane < 48, first, jnp.where(lane < 96, second, third))

    return (
        packed(score_t[0:16], pltpu.roll(score_t[16:32], 48, 1), pltpu.roll(score_t[32:48], 64, 1)),
        packed(pltpu.roll(score_t[48:64], 80, 1), score_t[64:80], pltpu.roll(score_t[80:96], 16, 1)),
    )


def unpack_scores(one, two):
    return jnp.concatenate(
        [one, pltpu.roll(one, 80, 1), pltpu.roll(one, 64, 1), pltpu.roll(two, 48, 1), two, pltpu.roll(two, 112, 1)],
        axis=0,
    )


def product_pair(score, score_t, x_of, go_of):
    pad = jnp.zeros((LANES - PAIR, LANES), BF16)
    low_half = lax.broadcasted_iota(jnp.int32, (PAIR, LANES), 1) < 64

    def halves(rows):
        zero = jnp.zeros_like(rows)
        return jnp.concatenate([jnp.where(low_half, rows, zero), jnp.where(low_half, zero, rows)], axis=0)

    by_i, by_j = [], []
    for duo in range(4):
        x, go = x_of(duo), go_of(duo)
        wide = lax.dot_general(halves(go), jnp.concatenate([x, pad], axis=0), NT, preferred_element_type=F32)
        wide_t = lax.dot_general(halves(x), jnp.concatenate([go, pad], axis=0), NT, preferred_element_type=F32)
        for part in range(2):
            by_i.append(wide[part * PAIR : (part + 1) * PAIR] * score)
            by_j.append(wide_t[part * PAIR : (part + 1) * PAIR] * score_t)
    return by_i, by_j


def mixer_pair(pre, by_i, by_j, rate, bias):
    lane = lanes()
    row = lax.broadcasted_iota(jnp.int32, (8, LANES), 0)
    gate = jnp.where(lane < PAIR, pre + bias, 0.0)
    e = jnp.exp(-jnp.abs(gate))
    series = e * (1.0 - e * (0.5 - e * (1.0 / 3.0 - e * (0.25 - e * 0.2))))
    log1p = jnp.where(e < 0.02, series, jnp.log(1.0 + e))
    step = jnp.maximum(gate, 0.0) + log1p
    sig = jnp.where(gate >= 0, 1.0, e) / (1.0 + e)
    level = exact_dot(jnp.where(lane < PAIR, -step * rate, 0.0), triangle("ahead"))
    cols = columns_of(level, step)
    away, away_t = causal(False), causal(True)
    grad_step = jnp.zeros((8, LANES), F32)
    outflow = jnp.zeros((8, LANES), F32)
    for head in range(8):
        level_col = cols[:PAIR, head : head + 1]
        step_col = cols[:PAIR, 8 + head : 9 + head]
        level_row = level[head : head + 1]
        weighted = by_i(head) * jnp.exp(level_col - level_row + away)
        flow = by_j(head) * jnp.exp(level_row - level_col + away_t) * step_col
        grad_step = jnp.where(row == head, jnp.sum(weighted, axis=0, keepdims=True), grad_step)
        outflow = jnp.where(row == head, jnp.sum(flow, axis=0, keepdims=True), outflow)
    grad_log = exact_dot(outflow - grad_step * step, triangle("behind"))
    return (grad_step - rate * grad_log) * sig, level, step


def per_head(ref, first_head):
    row = lax.broadcasted_iota(jnp.int32, (8, LANES), 0)
    out = jnp.zeros((8, LANES), F32)
    for head in range(8):
        out = jnp.where(row == head, ref[first_head + head], out)
    return out


def main_kernel(
    grid, n_block,
    tokens_any, w_ref, x_any, go_any, b_any, c_any, starts_ref, plan_ref, bias_ref, rate_ref,
    got_ref, notes_ref, dw_ref,
    stage_ref, xg_ref, wo_ref, full_ref, part_ref, rs_ref, give_ref, take_ref,
    x_ref, go_ref, b_ref, c_ref, send_ref, pre_ref, segs_ref, score_ref, score_t_ref, tile_ref, level_ref, note_ref,
    by_i_ref, by_j_ref, label_ref, gps_ref, half_ref, swap_ref, msg_ref, all_ref, heads_ref, xt_ref, d_ref, e1_ref, a1_ref, e2_ref,
    local_sem, load_sem, vs_sem, vr_sem, ts_sem, tr_sem, ps_sem, pr_sem, ss_sem, sr_sem,
    es_sem, er_sem, qs_sem, qr_sem, ns_sem, nr_sem, ws_sem, wr_sem, gs_sem, gr_sem, cs_sem, cr_sem, xs_sem, xr_sem,
    hs_sem, hr_sem, ks_sem, kr_sem, own_sem,
):
    n_z, n_x, n_y, n_dp = grid.n_z, grid.n_x, grid.n_y, grid.n_dp
    dp, yy, xx, core, yh, z = grid.here()
    shard = yh * n_z + z
    other = (1 - yh) * n_z + z
    across = {"shard": other}
    sibling = {"dp": grid.dp_of(yy, xx, 1 - core)}
    feats = w_ref.shape[0]
    per_half = n_z // 2

    def at_z(step):
        return {"shard": yh * n_z + (z + step) % n_z}

    def at_xy(side, step_x, step_y):
        place = grid.dp_of((yy + step_y) % n_y, (xx + step_x) % n_x, core)
        return {"dp": place, "shard": shard if side == 0 else other}

    plane = [(step_x, step_y) for step_x in range(n_x) for step_y in range(n_y)]

    barrier = pltpu.get_barrier_semaphore()
    for step in range(1, n_z):
        pl.semaphore_signal(barrier, inc=1, device_id=at_z(step), device_id_type=MESH)
    for step_x, step_y in plane:
        pl.semaphore_signal(barrier, inc=1, device_id=at_xy(1, step_x, step_y), device_id_type=MESH)

    @pl.loop(0, n_dp - 1)
    def _(s):
        pl.semaphore_signal(barrier, inc=1, device_id={"dp": grid.partner(s)}, device_id_type=MESH)

    def feature_columns(side, step):
        owner = (yh if side == 0 else 1 - yh) * n_z + (z + step) % n_z
        return tokens_any.at[:, pl.ds(pl.multiple_of(owner * feats, feats), feats)]

    group = (shard * 8) // (2 * n_z * 8 // G)
    cols = pl.ds(pl.multiple_of(group * N, N), N)
    staged = []
    for step in range(n_z):
        for side in range(2):
            target = stage_ref.at[step, side] if step else xg_ref.at[z, side]
            staged.append(pltpu.make_async_copy(feature_columns(side, step), target, local_sem.at[step, side]))
    for copy in staged:
        copy.start()
    loads = [
        pltpu.make_async_copy(b_any.at[:, :, cols], b_ref, load_sem.at[2]),
        pltpu.make_async_copy(c_any.at[:, :, cols], c_ref, load_sem.at[3]),
        pltpu.make_async_copy(go_any, go_ref, load_sem.at[1]),
        pltpu.make_async_copy(x_any, x_ref, load_sem.at[0]),
    ]
    for copy in loads:
        copy.start()
    pl.semaphore_wait(barrier, n_dp - 1 + n_z - 1 + n_x * n_y)

    mirrored = {"dp": grid.dp_of(n_y - 1 - yy, xx, core), "shard": other}
    weight_swap = remote(w_ref, wo_ref, vs_sem, vr_sem, mirrored)
    weight_swap.start()
    for copy in staged:
        copy.wait()
    token_copies = []
    for step in range(1, n_z):
        copy = remote(stage_ref.at[step], xg_ref.at[z], ts_sem.at[step], tr_sem.at[step], at_z(step))
        copy.start()
        token_copies.append(copy)

    def label_of(s):
        target = grid.partner(s)
        label = jnp.int32(0)
        for block in range(n_block):
            label = label + jnp.where(plan_ref[block] == target, block + 1, 0)
        return label

    def outgoing(s):
        body = pl.ds(0, TILES - 1)
        return remote(
            send_ref.at[s, body], got_ref.at[s, body], es_sem.at[s], er_sem.at[s], {"dp": grid.partner(s)}
        )

    def scored(s):
        return remote(
            send_ref.at[s, TILES - 1], got_ref.at[s, TILES - 1], qs_sem.at[s], qr_sem.at[s], {"dp": grid.partner(s)}
        )

    def noted(s):
        return remote(note_ref.at[s], notes_ref.at[s], ns_sem.at[s], nr_sem.at[s], {"dp": grid.partner(s)})

    def place(s):
        label = label_of(s)
        label_ref[s] = label
        whole = go_ref[jnp.clip(label - 1, 0, n_block - 1)]
        for r in range(3):
            for t in range(4):
                send_ref[s, 4 * r + t] = whole[16 * r : 16 * r + 16, t * LANES : (t + 1) * LANES]

    n_far = n_dp // 2

    def spans(index):
        for low, count, ends in ((0, n_far, FAR_ENDS), (n_far, n_dp - 1 - n_far, NEAR_ENDS)):
            begin = low + (ends[index - 1] * count // ends[-1] if index else 0)
            end = low + ends[index] * count // ends[-1]
            if end > begin:
                yield begin, end

    def batch(index):
        for begin, end in spans(index):
            @pl.loop(begin, end)
            def _(s):
                outgoing(s).start()

    loads[2].wait()
    for begin, end in spans(0):
        @pl.loop(begin, end)
        def _(s):
            place(s)
            outgoing(s).start()

    for index in (1, 2, 3):
        for begin, end in spans(index):
            @pl.loop(begin, end)
            def _(s):
                place(s)

    place(n_dp - 1)

    for copy in loads[:2]:
        copy.wait()
    rows = starts_ref[...].astype(F32)
    marks = jnp.concatenate(
        [jnp.broadcast_to(rows[r : r + 1], (8, rows.shape[1])) for r in range(rows.shape[0])], axis=1
    )
    for q in range(n_block // 2):
        segs_ref[q] = spread_lanes(marks, q * PAIR)

    def both(ref, q, low):
        return jnp.concatenate([ref[2 * q, :, pl.ds(low, LANES)], ref[2 * q + 1, :, pl.ds(low, LANES)]], axis=0)

    @pl.loop(0, n_block // 2)
    def _(q):
        score, score_t = score_pair(segs_ref[q], both(b_ref, q, 0), both(c_ref, q, 0))
        score_ref[q] = score
        score_t_ref[q] = score_t
        one, two = pack_scores(score_t)
        tile_ref[2 * q] = one.astype(BF16)
        tile_ref[2 * q + 1] = two.astype(BF16)

    @pl.loop(0, n_dp)
    def _(s):
        send_ref[s, TILES - 1] = tile_ref[jnp.clip(label_ref[s] - 1, 0, n_block - 1)]

        @pl.when(s < n_dp - 1)
        def _():
            scored(s).start()

    own = pltpu.make_async_copy(send_ref.at[n_dp - 1], got_ref.at[n_dp - 1], own_sem.at[0])
    own.start()

    w_here = w_ref[...].astype(F32).T.astype(BF16)
    for copy in loads[3:]:
        copy.wait()

    @pl.loop(0, n_block // 2)
    def _(q):
        by_i, by_j = product_pair(
            score_ref[q], score_t_ref[q],
            lambda duo: both(x_ref, q, duo * LANES), lambda duo: both(go_ref, q, duo * LANES),
        )
        for head in range(8):
            by_i_ref[q, head] = by_i[head]
            by_j_ref[q, head] = by_j[head]

    weight_swap.wait()
    w_other = wo_ref[...].astype(F32).T.astype(BF16)
    for copy in token_copies:
        copy.wait()
    columns = [xg_ref[:, side].reshape(n_z * BLK, feats) for side in range(2)]
    full_ref[...] = lax.dot_general(w_here, columns[0], NT, preferred_element_type=F32) + lax.dot_general(
        w_other, columns[1], NT, preferred_element_type=F32
    )
    copies = []
    for step in list(range(1, n_z)) + [0]:
        for side in range(2):
            owner = (yh if side == 0 else 1 - yh) * n_z + (z + step) % n_z
            part_ref[step, side * 8 : (side + 1) * 8] = full_ref[pl.ds(pl.multiple_of(owner * 8, 8), 8)]
        if step:
            copy = remote(part_ref.at[step], rs_ref.at[step], ps_sem.at[step], pr_sem.at[step], at_z(step))
            copy.start()
            copies.append(copy)
    for side in range(2):
        xt_ref[side] = columns[side].astype(F32).T.astype(BF16)
    total = part_ref[0]
    for step, copy in enumerate(copies, 1):
        copy.wait()
        total = total + rs_ref[step]
    give_ref[...] = total[8:]
    logit_swap = remote(give_ref, take_ref, ss_sem, sr_sem, across)
    logit_swap.start()
    for q in range(per_half):
        pre_ref[yh * per_half + q] = spread_lanes(total[:8], q * PAIR)

    rate = per_head(rate_ref, shard * 8)
    bias = per_head(bias_ref, shard * 8)
    lane = lanes()

    def work(*pairs):
        done = [
            mixer_pair(
                pre_ref[q], lambda head, q=q: by_i_ref[q, head], lambda head, q=q: by_j_ref[q, head], rate, bias
            )
            for q in pairs
        ]
        for q, (grad_pre, level, step) in zip(pairs, done):
            gps_ref[q] = grad_pre
            level_ref[2 * q] = jnp.where(lane < BLK, level, pltpu.roll(step, BLK, 1))
            level_ref[2 * q + 1] = jnp.where(lane < BLK, pltpu.roll(level, LANES - BLK, 1), step)

    def work_span(low, count):
        if count % 2:
            @pl.loop(0, count)
            def _(q):
                work(low + q)
        elif count:
            @pl.loop(0, count // 2)
            def _(q):
                work(low + 2 * q, low + 2 * q + 1)

    work_span(yh * per_half, per_half // 2)
    logit_swap.wait()
    others = take_ref[...]
    for q in range(per_half):
        pre_ref[(1 - yh) * per_half + q] = spread_lanes(others, q * PAIR)

    batch(1)
    work_span((1 - yh) * per_half, per_half)

    half_ref[0] = gather_lanes([gps_ref[(1 - yh) * per_half + i] for i in range(per_half)])
    grad_swap = remote(half_ref.at[0], swap_ref, ws_sem, wr_sem, across)
    grad_swap.start()

    work_span(yh * per_half + per_half // 2, per_half - per_half // 2)

    mine_half = gather_lanes([gps_ref[yh * per_half + i] for i in range(per_half)])
    grad_swap.wait()
    msg_ref[...] = jnp.concatenate([mine_half, swap_ref[...]], axis=0).astype(BF16)
    copies = []
    for step in range(1, n_z):
        copy = remote(msg_ref, all_ref.at[step], gs_sem.at[step], gr_sem.at[step], at_z(step))
        copy.start()
        copies.append(copy)

    batch(2)

    @pl.loop(0, n_dp)
    def _(s):
        label = label_ref[s]
        note_ref[s] = jnp.where(lane < PAIR, level_ref[jnp.clip(label - 1, 0, n_block - 1)], label.astype(F32))

        @pl.when(s < n_dp - 1)
        def _():
            noted(s).start()

    own_note = pltpu.make_async_copy(note_ref.at[n_dp - 1], notes_ref.at[n_dp - 1], own_sem.at[1])
    own_note.start()

    for step in range(n_z):
        if step:
            copies[step - 1].wait()
        message = (all_ref[step] if step else msg_ref[...]).astype(F32)
        place = (z + n_z - step) % n_z
        heads_ref[yh, place] = message[:8]
        heads_ref[1 - yh, place] = message[8:]
    grad_heads = heads_ref[...].reshape(2 * n_z * 8, heads_ref.shape[-1]).astype(BF16)
    unit = dw_ref.shape[0] // n_dp
    piece = n_y * unit
    for side in range(2):
        product = lax.dot_general(xt_ref[side], grad_heads, NT, preferred_element_type=F32)
        for c in range(2):
            for x in range(n_x):
                for y in range(n_y):
                    low = ((c * n_x + x) * n_y + y) * unit
                    d_ref[c, x, y, side] = product[low : low + unit]
    copy = remote(d_ref.at[1 - core], e1_ref, cs_sem, cr_sem, sibling)
    copy.start()
    copy.wait()
    a1_ref[...] = d_ref[core] + e1_ref[...]
    copies = []
    for step_x, step_y in plane[::-1]:
        for side in (1, 0):
            if side or step_x or step_y:
                copy = remote(
                    a1_ref.at[(xx + step_x) % n_x, (yy + step_y) % n_y, side], e2_ref.at[step_x, step_y, side],
                    xs_sem.at[step_x, step_y, side], xr_sem.at[step_x, step_y, side], at_xy(side, step_x, step_y),
                )
                copy.start()
                copies.append((step_x, step_y, side, copy))
    total = a1_ref[xx, yy, 0]
    for step_x, step_y, side, copy in copies:
        copy.wait()
        total = total + e2_ref[step_x, step_y, side]
    side_rows = n_x * piece
    low = pl.multiple_of(core * side_rows, side_rows)
    mine = pl.ds(pl.multiple_of(low + (xx * n_y + yy) * unit, unit), unit)
    dw_ref[mine] = total * (float(n_dp * n_block * BLK) ** -0.5)
    copies = []
    for step_x, step_y in plane[:0:-1]:
        copy = remote(
            dw_ref.at[mine], dw_ref.at[mine], hs_sem.at[step_x, step_y], hr_sem.at[step_x, step_y],
            at_xy(0, step_x, step_y),
        )
        copy.start()
        copies.append(copy)
    batch(3)
    for copy in copies:
        copy.wait()
    mine = pl.ds(low, side_rows)
    copy = remote(dw_ref.at[mine], dw_ref.at[mine], ks_sem, kr_sem, sibling)
    copy.start()
    copy.wait()

    @pl.loop(0, n_dp - 1)
    def _(s):
        scored(s).wait()
        noted(s).wait()
        outgoing(s).wait()

    own.wait()
    own_note.wait()


def main_call(grid, tokens, weight, x, go, b, c, starts, plan, bias, rate):
    n_block, _, width = x.shape
    n_z, n_x, n_y, n_dp = grid.n_z, grid.n_x, grid.n_y, grid.n_dp
    half = n_z * BLK
    feats, heads = weight.shape
    unit = feats // n_dp
    n_pair = n_block // 2
    dma = pltpu.SemaphoreType.DMA
    vmem = pl.BlockSpec(memory_space=pltpu.VMEM)
    smem = pl.BlockSpec(memory_space=pltpu.SMEM)
    hbm = pl.BlockSpec(memory_space=pl.ANY)
    return pl.pallas_call(
        functools.partial(main_kernel, grid, n_block),
        out_shape=(
            jax.ShapeDtypeStruct((n_dp, TILES, 16, LANES), BF16),
            jax.ShapeDtypeStruct((n_dp, 8, LANES), F32),
            jax.ShapeDtypeStruct((feats, heads), F32),
        ),
        in_specs=[hbm, vmem, hbm, hbm, hbm, hbm, vmem, smem, smem, smem],
        out_specs=[hbm, hbm, vmem],
        scratch_shapes=[
            pltpu.VMEM((n_z, 2, BLK, feats), BF16),
            pltpu.VMEM((n_z, 2, BLK, feats), BF16),
            pltpu.VMEM((feats, heads), BF16),
            pltpu.VMEM((heads, half), F32),
            pltpu.VMEM((n_z, 16, half), F32),
            pltpu.VMEM((n_z, 16, half), F32),
            pltpu.VMEM((8, half), F32),
            pltpu.VMEM((8, half), F32),
            pltpu.VMEM((n_block, BLK, width), BF16),
            pltpu.VMEM((n_block, BLK, width), BF16),
            pltpu.VMEM((n_block, BLK, N), BF16),
            pltpu.VMEM((n_block, BLK, N), BF16),
            pltpu.VMEM((n_dp, TILES, 16, LANES), BF16),
            pltpu.VMEM((n_pair, 8, LANES), F32),
            pltpu.VMEM((n_pair, 8, LANES), F32),
            pltpu.VMEM((n_pair, PAIR, LANES), F32),
            pltpu.VMEM((n_pair, PAIR, LANES), F32),
            pltpu.VMEM((n_block, 16, LANES), BF16),
            pltpu.VMEM((n_block, 8, LANES), F32),
            pltpu.VMEM((n_dp, 8, LANES), F32),
            pltpu.VMEM((n_pair, 8, PAIR, LANES), F32),
            pltpu.VMEM((n_pair, 8, PAIR, LANES), F32),
            pltpu.SMEM((n_dp,), jnp.int32),
            pltpu.VMEM((n_pair, 8, LANES), F32),
            pltpu.VMEM((1, 8, half), F32),
            pltpu.VMEM((8, half), F32),
            pltpu.VMEM((16, half), BF16),
            pltpu.VMEM((n_z, 16, half), BF16),
            pltpu.VMEM((2, n_z, 8, half), F32),
            pltpu.VMEM((2, feats, half), BF16),
            pltpu.VMEM((2, n_x, n_y, 2, unit, heads), F32),
            pltpu.VMEM((n_x, n_y, 2, unit, heads), F32),
            pltpu.VMEM((n_x, n_y, 2, unit, heads), F32),
            pltpu.VMEM((n_x, n_y, 2, unit, heads), F32),
            dma((n_z, 2)), dma((4,)), dma, dma, dma((n_z,)), dma((n_z,)), dma((n_z,)), dma((n_z,)), dma, dma,
            dma((n_dp,)), dma((n_dp,)), dma((n_dp,)), dma((n_dp,)), dma((n_dp,)), dma((n_dp,)), dma, dma, dma((n_z,)), dma((n_z,)), dma, dma,
            dma((n_x, n_y, 2)), dma((n_x, n_y, 2)), dma((n_x, n_y)), dma((n_x, n_y)), dma, dma, dma((2,)),
        ],
        compiler_params=pltpu.CompilerParams(
            collective_id=0, has_side_effects=True, vmem_limit_bytes=60 * 1024 * 1024
        ),
        cost_estimate=pl.CostEstimate(flops=10**9, bytes_accessed=10**7, transcendentals=10**6),
    )(tokens, weight, x, go, b, c, starts, plan, bias, rate)


def finish_kernel(gain_ref, got_ref, note_ref, dw_in_ref, out_ref, dw_ref, source_ref):
    shard = lax.axis_index("shard")
    lane = lanes()
    n_slot, n_block = got_ref.shape[0], out_ref.shape[0]
    labels = note_ref[:, 0, :]
    slot = lax.broadcasted_iota(jnp.int32, labels.shape, 0).astype(F32)
    labels = jnp.where(lax.broadcasted_iota(jnp.int32, labels.shape, 1) == LANES - 1, labels, 0.0)
    for block in range(n_block):
        found = jnp.sum(jnp.where(labels == float(block + 1), slot, 0.0))
        source_ref[block] = jnp.clip(found.astype(jnp.int32), 0, n_slot - 1)
    dw_ref[...] = dw_in_ref[...]
    away_t = causal(True)
    pad = jnp.zeros((LANES - PAIR, LANES), BF16)
    low_half = lax.broadcasted_iota(jnp.int32, (PAIR, LANES), 1) < 64

    def formed(q):
        first, second = source_ref[2 * q], source_ref[2 * q + 1]
        one, two = note_ref[first], note_ref[second]
        level = jnp.where(lane < BLK, one, jnp.where(lane < PAIR, pltpu.roll(two, BLK, 1), 0.0))
        step = jnp.where(lane < BLK, pltpu.roll(one, LANES - BLK, 1), jnp.where(lane < PAIR, two, 0.0))
        cols = columns_of(level, step)
        score_t = unpack_scores(
            got_ref[first, TILES - 1].astype(F32), got_ref[second, TILES - 1].astype(F32)
        )
        grads = []
        for duo in range(4):
            mix_t = []
            for head in (2 * duo, 2 * duo + 1):
                level_col = cols[:PAIR, head : head + 1]
                step_col = cols[:PAIR, 8 + head : 9 + head]
                mix_t.append(
                    (score_t * jnp.exp(level[head : head + 1] - level_col + away_t) * step_col).astype(BF16)
                )
            go = jnp.concatenate(
                [got_ref[first, 4 * r + duo] for r in range(3)] + [got_ref[second, 4 * r + duo] for r in range(3)],
                axis=0,
            )
            gv = lax.dot_general(
                jnp.concatenate(mix_t, axis=0), jnp.concatenate([go, pad], axis=0), NN, preferred_element_type=F32
            )
            gv = jnp.where(low_half, gv[:PAIR], gv[PAIR:])
            gain = jnp.where(low_half, gain_ref[shard * 8 + 2 * duo], gain_ref[shard * 8 + 2 * duo + 1])
            grads.append((gv + gain * go.astype(F32)).astype(BF16))
        return grads

    width = 2 if n_block % 4 == 0 else 1

    @pl.loop(0, n_block // 2 // width)
    def _(k):
        pairs = [width * k + i for i in range(width)]
        done = [formed(q) for q in pairs]
        for q, grads in zip(pairs, done):
            for duo, grad in enumerate(grads):
                out_ref[2 * q, :, duo * LANES : (duo + 1) * LANES] = grad[:BLK]
                out_ref[2 * q + 1, :, duo * LANES : (duo + 1) * LANES] = grad[BLK:]


def finish(gain, got, notes, dw, n_block):
    vmem = pl.BlockSpec(memory_space=pltpu.VMEM)
    smem = pl.BlockSpec(memory_space=pltpu.SMEM)
    return pl.pallas_call(
        finish_kernel,
        out_shape=(
            jax.ShapeDtypeStruct((n_block, BLK, 4 * LANES), BF16),
            jax.ShapeDtypeStruct(dw.shape, F32),
        ),
        in_specs=[smem, vmem, vmem, vmem],
        out_specs=[vmem, vmem],
        scratch_shapes=[pltpu.SMEM((n_block,), jnp.int32)],
        compiler_params=pltpu.CompilerParams(vmem_limit_bytes=60 * 1024 * 1024),
        cost_estimate=pl.CostEstimate(flops=10**8, bytes_accessed=4 * 10**6, transcendentals=10**6),
    )(gain, got, notes, dw)


def on_device(
    residual_in, conv_out, b_proj, c_proj, grad_out, doc_starts, dest_plan, dt_weight, dt_bias, decay_rate, skip_gain
):
    n_data = lax.axis_size("dp")
    grid = Grid(n_data, lax.axis_size("shard"))
    rows = conv_out.shape[0]
    n_block = rows // BLK

    def blocked(values):
        return values.reshape(n_block, BLK, -1)

    got, notes, dw = main_call(
        grid, residual_in, dt_weight, blocked(conv_out), blocked(grad_out), blocked(b_proj), blocked(c_proj),
        doc_starts.reshape(-1, math.gcd(rows, LANES)), dest_plan, dt_bias, decay_rate,
    )
    conv_grad, dw = finish(skip_gain, got, notes, dw, n_block)
    return conv_grad.reshape(rows, -1), dw


def solution(mesh):
    placed = (
        P(("dp", "shard"), None),
        P("dp", "shard"),
        P("dp", None),
        P("dp", None),
        P("dp", "shard"),
        P("dp"),
        P("dp"),
        P("shard", None),
        P(),
        P(),
        P(),
    )
    return jax.shard_map(
        on_device,
        mesh=mesh,
        in_specs=placed,
        out_specs=(P("dp", "shard"), P("shard", None)),
        check_vma=False,
    )
```
